256 devices in a mesh: dp: 4 (over y), ep: 64 (over z, x, core).
Axes of the slice: x: 4, y: 4, z: 8, core: 2. Of those that a mesh axis runs over, the one named last changes fastest.
Arguments:
- queries: bfloat16 [2048, 4096], P(('dp', 'ep')), may hold values from -12 to 12
- key_cache: bfloat16 [2048, 64, 256], P(('dp', 'ep')), may hold values from -6 to 6
- value_cache: bfloat16 [2048, 64, 256], P(('dp', 'ep')), may hold values from -6 to 6
- new_keys: bfloat16 [2048, 256], P(('dp', 'ep')), may hold values from -6 to 6
- new_values: bfloat16 [2048, 256], P(('dp', 'ep')), may hold values from -6 to 6
- cache_lengths: int32 [2048], P(('dp', 'ep')), may hold values from 2 to 63, as said below
- residual: bfloat16 [2048, 4096], P(('dp', 'ep')), may hold values from -6 to 6
- move_plan: int32 [2048, 2], P(('dp', 'ep')), may hold values from 0 to 2047, as said below
- norm_gain: float32 [4096], replicated, may hold values from 0.5 to 1.5
- expert_ids: int32 [2048, 8], P(('dp', 'ep')), may hold values from 0 to 63, all different within a row; in each aligned block of 8 rows (0 to 7, 8 to 15, ...) at most 2 rows name the same one
- gate_weights: float32 [2048, 8], P(('dp', 'ep')), may hold values from 0.1 to 1
- w_gate: bfloat16 [64, 4096, 1536], P('ep', None, 'dp'), may hold values from -0.09375 to 0.09375
- w_up: bfloat16 [64, 4096, 1536], P('ep', None, 'dp'), may hold values from -0.09375 to 0.09375
- w_down: bfloat16 [64, 1536, 4096], P('ep', 'dp'), may hold values from -0.15625 to 0.15625
Outputs:
- layer_out: bfloat16 [2048, 4096], P(('dp', 'ep'))
- keys_out: bfloat16 [2048, 64, 256], P(('dp', 'ep'))
- values_out: bfloat16 [2048, 64, 256], P(('dp', 'ep'))
The draws below stay inside these ranges and needn't reach their ends.
Inputs may be any that keep to these rules, and one draw needn't show every extreme that they name: `move_plan`: requests move only between devices of the same index of dp. Exactly 2 requests leave each device: for each d < 2, one goes to the device 1 + d * 31 indices further along ep (wrapping around), and exactly 2 arrive at each device, one from each of the devices that many indices before it, into the slots that it vacates. Column 0 names the slot whose request a slot holds after the move (itself if it stays), column 1 the slot that its own request moves to (itself if it stays). `cache_lengths`: every device's 8 requests include one of length 63. `expert_ids`: within the 8 rows of one device no expert is named by more than 2 rows, a bound that some block reaches.
All inputs are finite; a program needn't handle non-finite values.
Results may differ from the reference program's by a relative error of at most 0.011.
Values may be sent and summed in bfloat16 or wider, within the bound.
No kernel may reach another device: no remote copies, remote signals or barrier semaphores. Data moves between devices by JAX's collectives and lax.ppermute only.
A program may use at most 128 MiB of HBM per device.

```python
import math
import jax
import jax.numpy as jnp
import numpy as np
from jax import lax

D = 4096
HD = 128
QH = 32
KVH = 2
FF = 1536
TOP = 8
MIG = 2
REQ_DEV = 8
SLOT = 64
EXPERTS = 64
MOST = 2
REQUESTS = 2048
N_DP = 4
N_EP = 64


def draw_key_cache(key, part):
    key = jax.random.fold_in(key, 7)
    cache_keys = jnp.clip(jax.random.normal(key, (REQUESTS, SLOT, KVH * HD), jnp.float32), -6.0, 6.0)
    return cache_keys.astype(jnp.bfloat16)


def draw_queries(key, part):
    key = jax.random.fold_in(key, 9)
    query_rows = jnp.clip(jax.random.normal(key, (REQUESTS, QH * HD), jnp.float32), -12.0, 12.0)
    return query_rows.astype(jnp.bfloat16)


def draw_cache_lengths(key, part):
    key = jax.random.fold_in(key, 3)
    first_draw = jax.random.randint(jax.random.fold_in(key, 1), (REQUESTS,), 2, SLOT)
    second_draw = jax.random.randint(jax.random.fold_in(key, 2), (REQUESTS,), 2, SLOT)
    lengths = jnp.minimum(first_draw, second_draw)
    longest_at = jax.random.randint(jax.random.fold_in(key, 4), (REQUESTS // REQ_DEV,), 0, REQ_DEV)
    marked = jnp.arange(REQUESTS, dtype=jnp.int32) % REQ_DEV == jnp.repeat(longest_at, REQ_DEV)
    return jnp.where(marked, SLOT - 1, lengths).astype(jnp.int32)


def draw_move_plan(key, part):
    key = jax.random.fold_in(key, 5)
    slot_keys = jax.random.split(jax.random.fold_in(key, 2), N_DP * N_EP)
    slot_order = jax.vmap(lambda one_key: jax.random.permutation(one_key, REQ_DEV))(slot_keys)
    slot_order = slot_order.astype(jnp.int32).reshape(N_DP, N_EP, REQ_DEV)
    row_index = jnp.arange(N_DP, dtype=jnp.int32)[:, None]
    column_index = jnp.arange(N_EP, dtype=jnp.int32)[None, :]
    everything = jnp.arange(N_DP * N_EP * REQ_DEV, dtype=jnp.int32).reshape(N_DP, N_EP, REQ_DEV)
    source = everything
    target = everything
    for offset in range(MIG):
        distance = 1 + offset * (N_EP // 2 - 1) // (MIG - 1)
        to_device = (column_index + distance) % N_EP
        from_device = (column_index - distance) % N_EP
        here_slot = slot_order[:, :, offset]
        to_slot = slot_order[row_index, to_device, offset]
        from_slot = slot_order[row_index, from_device, offset]
        target = target.at[row_index, column_index, here_slot].set((row_index * N_EP + to_device) * REQ_DEV + to_slot)
        source = source.at[row_index, column_index, here_slot].set((row_index * N_EP + from_device) * REQ_DEV + from_slot)
    return jnp.stack([source.reshape(-1), target.reshape(-1)], axis=1).astype(jnp.int32)


def levels(key, extent, pieces, low, high):
    def one(dim, shards_of):
        heights = jax.random.uniform(jax.random.fold_in(jax.random.fold_in(key, 6), dim), (shards_of,), jnp.float32, low / len(pieces), high / len(pieces))
        return jnp.repeat(jnp.exp(heights), extent[dim] // shards_of).reshape((-1,) + (1,) * (len(extent) - dim - 1))

    level = one(*pieces[0])
    for cut in pieces[1:]:
        level = level * one(*cut)
    return level


def assign_block(own_key, own, number, rows, number_of, top, limit, skew):
    ranking = jax.random.permutation(own_key, number_of)
    crowded, usual = shares(number_of, rows * top, limit, skew, True), shares(number_of, rows * top, limit, skew, False)
    places = jnp.arange(number_of)

    def named(sizes, rotation):
        used = int((sizes > 0).sum())
        fixed = max(1, used // 4)
        passed = fixed + (places - fixed + rotation * (used - fixed)) % max(1, number_of - fixed)
        return jnp.zeros((number_of,), jnp.int32).at[ranking[jnp.where(places < fixed, places, passed)]].set(jnp.asarray(sizes, jnp.int32))

    sizes = jnp.where(number % 4 == 0, named(crowded, number // 4), named(usual, number - number // 4 - 1))
    mixed = jax.random.permutation(jax.random.fold_in(own, 3), number_of)
    donor, taker = mixed[0:number_of // 2 * 2:2], mixed[1:number_of // 2 * 2:2]
    slack = jnp.minimum(sizes[donor] - 1, limit - sizes[taker]) // 2
    slack = jnp.where((donor == ranking[0]) | (taker == ranking[0]) | (sizes[taker] == 0), 0, jnp.maximum(slack, 0))
    passed = jax.random.randint(jax.random.fold_in(own, 4), (number_of // 2,), 0, 1 << 20) % (slack + 1)
    sizes = sizes.at[donor].add(-passed).at[taker].add(passed)
    labels = jnp.searchsorted(jnp.cumsum(sizes), jnp.arange(rows * top), side="right").astype(jnp.int32)
    grid = labels.reshape(top, rows).T
    grid = grid[jax.random.permutation(jax.random.fold_in(own, 1), rows)]
    rotation = jax.random.randint(jax.random.fold_in(own, 2), (rows, 1), 0, top)
    return jnp.take_along_axis(grid, (jnp.arange(top)[None, :] + rotation) % top, axis=1)


def shares(amount, total, bound, lean, full):
    portions = [(1 << 20) // math.isqrt(rank ** lean) + 1 for rank in range(1, amount + 1)]
    largest = bound if full else min(bound, max(-(-total // amount), total * portions[0] // sum(portions)))
    least = 1 if total - largest >= amount - 1 else 0
    counts, rest = [largest] + [least] * (amount - 1), total - largest - least * (amount - 1)
    while rest > 0:
        candidates = [i for i in range(1, amount) if counts[i] < largest] or [i for i in range(1, amount) if counts[i] < bound]
        whole, remaining = sum([portions[i] for i in candidates]), rest
        for i in candidates:
            extra = min(bound - counts[i], max(1, remaining * portions[i] // whole), rest)
            counts[i] = counts[i] + extra
            rest = rest - extra
    return np.array(counts)


def noise(own_key, dims, width, most, shards=(), kind=jnp.bfloat16):
    values = width * jax.random.normal(own_key, dims, jnp.float32)
    if shards:
        values = values * levels(own_key, dims, shards, -0.22, 0.18)
    return jnp.clip(values, -most, most).astype(kind)


def setup_inputs(seed: int = 0) -> dict:
    arg_keys = jax.random.split(jax.random.key(seed), 15)
    queries = draw_queries(jax.random.fold_in(arg_keys[14], 71), 0)
    key_cache = draw_key_cache(jax.random.fold_in(arg_keys[14], 71), 0)
    value_cache = noise(arg_keys[2], (REQUESTS, SLOT, KVH * HD), 1.0, 6.0, ((0, 256),))
    new_keys = noise(arg_keys[3], (REQUESTS, KVH * HD), 1.0, 6.0, ((0, 256),))
    new_values = noise(arg_keys[4], (REQUESTS, KVH * HD), 1.0, 6.0, ((0, 256),))
    cache_lengths = draw_cache_lengths(jax.random.fold_in(arg_keys[14], 71), 0)
    residual = noise(arg_keys[6], (REQUESTS, D), 1.0, 6.0, ((0, 256),))
    move_plan = draw_move_plan(jax.random.fold_in(arg_keys[14], 71), 0)
    norm_gain = jnp.clip(1.0 + 0.1 * jax.random.normal(arg_keys[8], (D,), jnp.float32), 0.5, 1.5)
    expert_ids_keys = jax.random.split(jax.random.fold_in(arg_keys[9], 1), REQUESTS // REQ_DEV)
    expert_ids_turns = jax.random.permutation(jax.random.fold_in(arg_keys[9], 3), REQUESTS // REQ_DEV)
    expert_ids = jax.vmap(lambda own, number: assign_block(jax.random.fold_in(arg_keys[9], 2), own, number, REQ_DEV, EXPERTS, TOP, MOST, 2))(expert_ids_keys, expert_ids_turns).reshape((REQUESTS, TOP))
    gate_weights = jnp.clip(jnp.exp(math.log(1.0) - 2.3025851 * jax.random.uniform(arg_keys[10], (REQUESTS, TOP), jnp.float32) ** levels(arg_keys[10], (REQUESTS, TOP), ((0, 256),), -0.2, 0.2)), 0.1, 1.0)
    w_gate = noise(arg_keys[11], (EXPERTS, D, FF), D ** -0.5, 0.09375, ((0, 64), (2, 4)))
    w_up = noise(arg_keys[12], (EXPERTS, D, FF), D ** -0.5, 0.09375, ((0, 64), (2, 4)))
    w_down = noise(arg_keys[13], (EXPERTS, FF, D), FF ** -0.5, 0.15625, ((0, 64), (1, 4)))
    return dict(queries=queries, key_cache=key_cache, value_cache=value_cache, new_keys=new_keys, new_values=new_values, cache_lengths=cache_lengths, residual=residual, move_plan=move_plan, norm_gain=norm_gain, expert_ids=expert_ids, gate_weights=gate_weights, w_gate=w_gate, w_up=w_up, w_down=w_down)


def expert_block(operands):
    expert_rows, gate_matrix, up_matrix, down_matrix = operands
    gate_proj = jnp.dot(expert_rows, gate_matrix, preferred_element_type=jnp.float32)
    up_proj = jnp.dot(expert_rows, up_matrix, preferred_element_type=jnp.float32)
    hidden = (jax.nn.silu(gate_proj) * up_proj).astype(jnp.bfloat16)
    unit_width = FF // N_DP
    accumulated = jnp.zeros((expert_rows.shape[0], D), jnp.float32)
    for replica in range(N_DP):
        partial_sum = jnp.dot(hidden[:, replica * unit_width:(replica + 1) * unit_width], down_matrix[replica * unit_width:(replica + 1) * unit_width], preferred_element_type=jnp.float32)
        rounded = lax.optimization_barrier(partial_sum.astype(jnp.bfloat16))
        accumulated = accumulated + rounded.astype(jnp.float32)
    return accumulated.astype(jnp.bfloat16)

def reference(queries, key_cache, value_cache, new_keys, new_values, cache_lengths, residual, move_plan, norm_gain, expert_ids, gate_weights, w_gate, w_up, w_down):
    source = move_plan[:, 0]
    total_requests = queries.shape[0]
    groups = QH // KVH
    lengths = cache_lengths[source]
    positions = jnp.arange(SLOT, dtype=jnp.int32)
    newest = (positions[None, :] == lengths[:, None])[:, :, None]
    keys_out = jnp.where(newest, new_keys[source][:, None, :], key_cache[source])
    values_out = jnp.where(newest, new_values[source][:, None, :], value_cache[source])
    query_heads = queries[source].astype(jnp.float32).reshape(total_requests, KVH, groups, HD)
    key_heads = keys_out.astype(jnp.float32).reshape(total_requests, SLOT, KVH, HD)
    value_heads = values_out.astype(jnp.float32).reshape(total_requests, SLOT, KVH, HD)
    scores = jnp.einsum('rkgd,rpkd->rkgp', query_heads, key_heads) * (1.0 / math.sqrt(HD))
    visible = (positions[None, :] <= lengths[:, None])[:, None, None, :]
    scores = jnp.where(visible, scores, -jnp.inf)
    highest = lax.optimization_barrier(jnp.max(scores, axis=-1, keepdims=True))
    weights = jnp.exp(scores - highest)
    probabilities = (weights / lax.optimization_barrier(jnp.sum(weights, axis=-1, keepdims=True))).astype(jnp.bfloat16)
    attended = jnp.einsum('rkgp,rpkd->rkgd', probabilities.astype(jnp.float32), value_heads)
    attended = attended.reshape(total_requests, D)
    summed = residual[source].astype(jnp.float32) + attended
    normed = (summed * lax.rsqrt(lax.optimization_barrier(jnp.mean(summed * summed, axis=-1, keepdims=True)) + 1e-06) * norm_gain).astype(jnp.bfloat16)
    routes = expert_ids.reshape(-1)
    count_routes = routes.shape[0]
    route_marks = (routes[:, None] == jnp.arange(EXPERTS, dtype=jnp.int32)[None, :]).astype(jnp.int32)
    before = jnp.cumsum(route_marks, axis=0) - route_marks
    route_place = lax.optimization_barrier(jnp.sum(before * route_marks, axis=1)).astype(jnp.int32)
    capacity = N_DP * N_EP * MOST
    slot_table = jnp.full((EXPERTS, capacity), count_routes, jnp.int32)
    slot_table = slot_table.at[routes, route_place].set(jnp.arange(count_routes, dtype=jnp.int32))
    padded = jnp.concatenate([normed, jnp.zeros((1, D), jnp.bfloat16)], axis=0)
    owner_rows = jnp.concatenate([jnp.arange(count_routes, dtype=jnp.int32) // TOP, jnp.full((1,), total_requests, jnp.int32)])
    gathered = padded[owner_rows[slot_table]]
    outputs = lax.map(expert_block, (gathered, w_gate, w_up, w_down))
    picked = outputs.reshape(EXPERTS * capacity, D)[routes * capacity + route_place]
    picked = picked.reshape(total_requests, TOP, D)
    mixture = lax.optimization_barrier(jnp.sum(gate_weights[:, :, None] * picked.astype(jnp.float32), axis=1))
    layer_out = (summed + mixture).astype(jnp.bfloat16)
    return (layer_out, keys_out, values_out)
```

```python
import math

import jax
import jax.numpy as jnp
from jax import lax
from jax.experimental import pallas as pl
from jax.experimental.pallas import tpu as pltpu
from jax.sharding import PartitionSpec as P

HD = 128
TOP = 8
MIG = 2
MOST = 2
COLS = 8
STEP = 512
F32 = jnp.float32
BF16 = jnp.bfloat16
VMEM = pl.BlockSpec(memory_space=pltpu.VMEM)
HBM = pl.BlockSpec(memory_space=pltpu.HBM)


def iota(shape, dim):
    return lax.broadcasted_iota(jnp.int32, shape, dim)


def one_hot(condition):
    return jnp.where(condition, 1.0, 0.0).astype(BF16)


def distances(ep_count):
    return tuple(1 + d * (ep_count // 2 - 1) for d in range(MIG))


def find_slot(plan_ref, column, rank, per_device, ep_count):
    found = jnp.int32(0)
    for r in range(per_device):
        other = lax.rem(lax.div(plan_ref[column, r], per_device), ep_count)
        found = jnp.where(other == rank, jnp.int32(r), found)
    return found


def attend_kernel(
    ep_count,
    lengths_ref,
    plan_ref,
    queries_ref,
    keys_ref,
    values_ref,
    new_keys_ref,
    new_values_ref,
    residual_ref,
    ids_ref,
    gain_ref,
    keys_out_ref,
    values_out_ref,
    carry_ref,
    row0_ref,
    row1_ref,
    cache0_ref,
    cache1_ref,
):
    requests, slots, width = keys_ref.shape
    heads = queries_ref.shape[1] // HD
    kv_heads = width // HD
    groups = heads // kv_heads
    fresh_keys = new_keys_ref[...].astype(F32)
    fresh_values = new_values_ref[...].astype(F32)
    position = iota((slots, width), 0)
    for r in range(requests):
        newest = position == lengths_ref[r]
        keys_out_ref[r] = jnp.where(
            newest, fresh_keys[r : r + 1], keys_ref[r].astype(F32)
        ).astype(BF16)
        values_out_ref[r] = jnp.where(
            newest, fresh_values[r : r + 1], values_ref[r].astype(F32)
        ).astype(BF16)
    total = requests * slots
    column = iota((groups * requests, total), 1)
    holder = lax.div(column, slots)
    limit = jnp.zeros_like(column)
    for r in range(requests):
        limit = jnp.where(holder == r, lengths_ref[r], limit)
    own_row = lax.rem(iota((groups * requests, total), 0), requests)
    visible = (holder == own_row) & (lax.rem(column, slots) <= limit)
    queries = queries_ref[...].astype(F32)
    residual = residual_ref[...].astype(F32)
    all_keys = keys_out_ref[...].reshape(total, width)
    all_values = values_out_ref[...].reshape(total, width)
    for k in range(kv_heads):
        stacked = jnp.concatenate(
            [
                queries[:, (k * groups + h) * HD : (k * groups + h + 1) * HD]
                for h in range(groups)
            ],
            axis=0,
        ).astype(BF16)
        scores = lax.dot_general(
            stacked,
            all_keys[:, k * HD : (k + 1) * HD],
            (((1,), (1,)), ((), ())),
            preferred_element_type=F32,
        ) * (1.0 / math.sqrt(HD))
        scores = jnp.where(visible, scores, -jnp.inf)
        weights = jnp.exp(scores - jnp.max(scores, axis=1, keepdims=True))
        probabilities = (weights / jnp.sum(weights, axis=1, keepdims=True)).astype(BF16)
        attended = jnp.dot(
            probabilities, all_values[:, k * HD : (k + 1) * HD], preferred_element_type=F32
        )
        for h in range(groups):
            place = slice((k * groups + h) * HD, (k * groups + h + 1) * HD)
            carry_ref[0:requests, place] = (
                residual[:, place] + attended[h * requests : (h + 1) * requests]
            )
    rank = lax.axis_index("ep")
    summed = carry_ref[0:requests]
    row_number = iota(summed.shape, 0)
    for d, (distance, row_ref, cache_ref) in enumerate(
        zip(distances(ep_count), (row0_ref, row1_ref), (cache0_ref, cache1_ref))
    ):
        slot = find_slot(plan_ref, 1, lax.rem(rank + distance, ep_count), requests, ep_count)
        row_ref[...] = jnp.sum(jnp.where(row_number == slot, summed, 0.0), axis=0, keepdims=True)
        cache_ref[0:slots] = keys_out_ref[slot]
        cache_ref[slots : 2 * slots] = values_out_ref[slot]
        origin = lax.rem(rank + ep_count - distance, ep_count)
        arrival = find_slot(plan_ref, 0, origin, requests, ep_count)
        carry_ref[2 * requests : 3 * requests, (2 + d) * HD : (3 + d) * HD] = jnp.where(
            iota((requests, HD), 0) == arrival, 1.0, 0.0
        )
    carry_ref[requests : 2 * requests] = jnp.broadcast_to(gain_ref[...], summed.shape)
    chosen, _, earlier = routes(ids_ref[...], None, ep_count)
    carry_ref[2 * requests : 3 * requests, 0:ep_count] = chosen
    carry_ref[2 * requests : 3 * requests, HD : HD + ep_count] = earlier


def routes(ids, gates, experts):
    rows = ids.shape[0]
    expert = iota((rows, experts), 1)
    chosen = jnp.zeros((rows, experts), F32)
    weight = jnp.zeros((rows, experts), F32)
    for k in range(TOP):
        same = ids[:, k : k + 1] == expert
        chosen = jnp.where(same, 1.0, chosen)
        if gates is not None:
            weight = jnp.where(same, gates[:, k : k + 1], weight)
    earlier = []
    running = jnp.zeros((1, experts), F32)
    for r in range(rows):
        earlier.append(running)
        running = running + chosen[r : r + 1]
    return chosen, weight, jnp.concatenate(earlier, axis=0)


def place_kernel(ep_count, carry_ref, row0_ref, row1_ref, summed_out_ref, slots_ref):
    rows, model_width = summed_out_ref.shape
    summed = carry_ref[0:rows]
    notes = slice(2 * rows, 3 * rows)
    for d, row_ref in enumerate((row0_ref, row1_ref)):
        arrival = carry_ref[notes, (2 + d) * HD : (2 + d) * HD + 1]
        summed = jnp.where(arrival > 0.5, row_ref[...], summed)
    summed_out_ref[...] = summed
    scale = lax.rsqrt(jnp.mean(summed * summed, axis=1, keepdims=True) + 1e-06)
    normed = summed * scale * carry_ref[rows : 2 * rows]
    part = model_width // COLS
    pieces = jnp.concatenate(
        [normed[:, c * part : (c + 1) * part] for c in range(COLS)], axis=0
    ).astype(BF16)
    chosen = carry_ref[notes, 0:ep_count]
    earlier = carry_ref[notes, HD : HD + ep_count]
    deep = MOST * COLS
    wide = (ep_count * deep, ep_count)
    spread = one_hot(lax.div(iota(wide, 0), deep) == iota(wide, 1))
    repeat_shape = (rows, COLS * rows)
    repeat = one_hot(iota(repeat_shape, 0) == lax.rem(iota(repeat_shape, 1), rows))
    pick_shape = (ep_count * deep, COLS * rows)
    row_here = iota(pick_shape, 0)
    same_part = lax.rem(row_here, COLS) == lax.div(iota(pick_shape, 1), rows)
    slot_here = lax.rem(lax.div(row_here, COLS), MOST)
    pick = jnp.zeros(pick_shape, F32)
    for s in range(MOST):
        placed = jnp.where(earlier == float(s), chosen, 0.0).astype(BF16)
        by_expert = lax.dot_general(
            placed, repeat, (((0,), (0,)), ((), ())), preferred_element_type=F32
        ).astype(BF16)
        by_piece = jnp.dot(spread, by_expert, preferred_element_type=F32)
        pick = jnp.where(same_part & (slot_here == s), by_piece, pick)
    slots_ref[...] = jnp.dot(pick.astype(BF16), pieces, preferred_element_type=F32).astype(BF16)


def regroup(rows):
    shape = (rows, rows)
    count = rows // COLS
    first = iota(shape, 0)
    return one_hot(
        iota(shape, 1) == lax.rem(first, count) * COLS + lax.div(first, count)
    )


def expert_kernel(n_pieces, n_blocks, *refs):
    piece_refs = refs[:n_pieces]
    gate_ref, up_ref, down_ref = refs[n_pieces : n_pieces + 3]
    out_refs = refs[n_pieces + 3 : n_pieces + 3 + n_blocks]
    rows_ref = refs[-1]
    model_width, hidden_width = gate_ref.shape[1:]
    count = STEP // COLS
    part = model_width // COLS
    order = regroup(STEP)
    n = 0
    for ref in piece_refs:
        for m in range(ref.shape[0] // STEP):
            sorted_rows = jnp.dot(
                order, ref[m * STEP : (m + 1) * STEP], preferred_element_type=F32
            ).astype(BF16)
            for c in range(COLS):
                rows_ref[n * count : (n + 1) * count, c * part : (c + 1) * part] = sorted_rows[
                    c * count : (c + 1) * count
                ]
            n += 1
    rows = rows_ref[...]
    gate_proj = jnp.dot(rows, gate_ref[0], preferred_element_type=F32)
    up_proj = jnp.dot(rows, up_ref[0], preferred_element_type=F32)
    hidden = (gate_proj / (1.0 + jnp.exp(-gate_proj)) * up_proj).astype(BF16)
    for c in range(COLS):
        term = jnp.dot(
            hidden, down_ref[0, :, c * part : (c + 1) * part], preferred_element_type=F32
        ).astype(BF16)
        for n in range(n_blocks):
            out_refs[n][c * count : (c + 1) * count] = term[n * count : (n + 1) * count]


def relay_kernel(right_ref, left_ref, from_left_ref, from_right_ref, to_right_ref, to_left_ref):
    to_right_ref[...] = (right_ref[...].astype(F32) + from_left_ref[...].astype(F32)).astype(BF16)
    to_left_ref[...] = (left_ref[...].astype(F32) + from_right_ref[...].astype(F32)).astype(BF16)


def gather_kernel(
    own_top_ref,
    own_bottom_ref,
    left_top_ref,
    left_bottom_ref,
    right_top_ref,
    right_bottom_ref,
    out_ref,
):
    order = regroup(STEP)
    for i, refs in enumerate(
        (
            (own_top_ref, left_top_ref, right_top_ref),
            (own_bottom_ref, left_bottom_ref, right_bottom_ref),
        )
    ):
        total = sum(ref[...].astype(F32) for ref in refs).astype(BF16)
        out_ref[i * STEP : (i + 1) * STEP] = lax.dot_general(
            order, total, (((0,), (0,)), ((), ())), preferred_element_type=F32
        ).astype(BF16)


def mix_kernel(ids_ref, gates_ref, summed_ref, returned_ref, out_ref):
    rows, model_width = summed_ref.shape
    deep = MOST * COLS
    experts = returned_ref.shape[0] // deep
    part = model_width // COLS
    chosen, weight, earlier = routes(ids_ref[...], gates_ref[...], experts)
    repeat_shape = (COLS * rows, rows)
    repeat = one_hot(lax.rem(iota(repeat_shape, 0), rows) == iota(repeat_shape, 1))
    wide = (experts, experts * deep)
    spread = one_hot(iota(wide, 0) == lax.div(iota(wide, 1), deep))
    pick_shape = (COLS * rows, experts * deep)
    column = iota(pick_shape, 1)
    same_part = lax.div(iota(pick_shape, 0), rows) == lax.rem(column, COLS)
    slot_here = lax.rem(lax.div(column, COLS), MOST)
    returned = returned_ref[...]
    coarse_pick = jnp.zeros(pick_shape, F32)
    fine_pick = jnp.zeros(pick_shape, F32)
    for s in range(MOST):
        placed = jnp.where((earlier == float(s)) & (chosen > 0.5), weight, 0.0)
        coarse = placed.astype(BF16)
        fine = (placed - coarse.astype(F32)).astype(BF16)
        here = same_part & (slot_here == s)
        by_row = jnp.dot(
            jnp.dot(repeat, coarse, preferred_element_type=F32).astype(BF16),
            spread,
            preferred_element_type=F32,
        )
        coarse_pick = jnp.where(here, by_row, coarse_pick)
        by_row = jnp.dot(
            jnp.dot(repeat, fine, preferred_element_type=F32).astype(BF16),
            spread,
            preferred_element_type=F32,
        )
        fine_pick = jnp.where(here, by_row, fine_pick)
    mixture = jnp.dot(coarse_pick.astype(BF16), returned, preferred_element_type=F32)
    mixture += jnp.dot(fine_pick.astype(BF16), returned, preferred_element_type=F32)
    for c in range(COLS):
        here = slice(c * part, (c + 1) * part)
        out_ref[:, here] = (
            summed_ref[:, here] + mixture[c * rows : (c + 1) * rows]
        ).astype(BF16)


def settle_kernel(
    ep_count,
    plan_ref,
    cache0_ref,
    cache1_ref,
    keys_in_ref,
    values_in_ref,
    keys_ref,
    values_ref,
    sems,
):
    del keys_in_ref, values_in_ref
    requests, slots, _ = keys_ref.shape
    rank = lax.axis_index("ep")
    copies = []
    for d, (distance, cache_ref) in enumerate(zip(distances(ep_count), (cache0_ref, cache1_ref))):
        origin = lax.rem(rank + ep_count - distance, ep_count)
        slot = find_slot(plan_ref, 0, origin, requests, ep_count)
        for i, ref in enumerate((keys_ref, values_ref)):
            copies.append(
                pltpu.make_async_copy(
                    cache_ref.at[pl.ds(i * slots, slots)], ref.at[slot], sems.at[d, i]
                )
            )
            copies[-1].start()
    for copy in copies:
        copy.wait()


def shape_of(shape, dtype):
    return jax.ShapeDtypeStruct(shape, dtype)


def call(kernel, outs, scalars, staged, resident, flops, moved, limit=16, scratch=()):
    n_scalars, n_staged, n_resident = map(len, (scalars, staged, resident))
    n_outs = len(outs) if isinstance(outs, tuple) else 1

    def body(*refs):
        refs = list(refs)

        def take(count):
            taken = refs[:count]
            del refs[:count]
            return taken

        scalar_refs, sources, resident_refs, out_refs = map(
            take, (n_scalars, n_staged, n_resident, n_outs)
        )
        own_refs = take(len(scratch))
        staged_refs = take(n_staged)
        copies = [
            pltpu.make_async_copy(source, target, refs[0].at[i])
            for i, (source, target) in enumerate(zip(sources, staged_refs))
        ]
        for copy in copies:
            copy.start()
        for copy in copies:
            copy.wait()
        kernel(*scalar_refs, *staged_refs, *resident_refs, *out_refs, *own_refs)

    stages = [pltpu.VMEM(arg.shape, arg.dtype) for arg in staged]
    if staged:
        stages.append(pltpu.SemaphoreType.DMA((n_staged,)))
    return pl.pallas_call(
        body,
        out_shape=outs,
        grid_spec=pltpu.PrefetchScalarGridSpec(
            num_scalar_prefetch=n_scalars,
            grid=(),
            in_specs=[HBM] * n_staged + [VMEM] * n_resident,
            out_specs=tuple([VMEM] * n_outs) if isinstance(outs, tuple) else VMEM,
            scratch_shapes=[*scratch, *stages],
        ),
        compiler_params=pltpu.CompilerParams(vmem_limit_bytes=limit * 2**20),
        cost_estimate=pl.CostEstimate(flops=flops, bytes_accessed=moved, transcendentals=0),
    )(*scalars, *staged, *resident)


def experts_of(pieces, weights):
    rows = sum(piece.shape[0] for piece in pieces)
    part = pieces[0].shape[1]
    n_blocks = rows // STEP
    model_width, hidden_width = weights[0].shape[1:]
    tokens = rows // COLS

    def kernel(*refs):
        expert_kernel(len(pieces), n_blocks, *refs)

    return call(
        kernel,
        tuple(shape_of((STEP, part), BF16) for _ in range(n_blocks)),
        (),
        (),
        (*pieces, *weights),
        6 * tokens * model_width * hidden_width,
        6 * model_width * hidden_width + 4 * rows * part,
        limit=20,
        scratch=[pltpu.VMEM((tokens, model_width), BF16)],
    )


def rotate(member, axis, distance):
    count = lax.axis_size(axis)
    return lax.ppermute(member, axis, [(s, (s + distance) % count) for s in range(count)])


def exchange(member):
    experts = lax.axis_size("ep")
    cut = member.reshape(experts, member.shape[0] // experts, member.shape[1])
    cut = lax.all_to_all(cut, "ep", split_axis=0, concat_axis=0, tiled=True)
    return cut.reshape(member.shape)


def after(member, *earlier):
    return lax.optimization_barrier((member, *earlier))[0]


def through_experts(own, weights, beside):
    from_left = rotate(own, "dp", 1)
    from_right = rotate(own, "dp", -1)
    own_top, own_bottom = experts_of([own], weights)
    from_left, from_right, own_top, own_bottom, *beside = lax.optimization_barrier(
        (from_left, from_right, own_top, own_bottom, *beside)
    )
    far_top = rotate(from_left[:STEP], "dp", 1)
    far_bottom = rotate(from_right[STEP:], "dp", -1)
    left_top, left_bottom, right_top, right_bottom = experts_of([from_left, from_right], weights)
    far_top, far_bottom, right_top, left_bottom = lax.optimization_barrier(
        (far_top, far_bottom, right_top, left_bottom)
    )
    direct_left = rotate(after(right_bottom, far_top, far_bottom), "dp", 1)
    direct_right = rotate(after(left_top, far_top, far_bottom), "dp", -1)
    far_terms = experts_of([far_top, far_bottom], weights)
    relayed_left = rotate(far_terms[0], "dp", 1)
    relayed_right = rotate(far_terms[1], "dp", -1)
    block = shape_of(far_top.shape, BF16)
    size = 2 * block.size
    to_right, to_left = call(
        relay_kernel,
        (block, block),
        (),
        (),
        (right_top, left_bottom, relayed_left, relayed_right),
        size,
        5 * size,
    )
    sums_left = rotate(to_right, "dp", 1)
    sums_right = rotate(to_left, "dp", -1)
    sums = call(
        gather_kernel,
        shape_of(own.shape, BF16),
        (),
        (),
        (own_top, own_bottom, sums_left, direct_left, direct_right, sums_right),
        2 * size * STEP,
        8 * size,
    )
    return sums, beside


def local(
    queries,
    key_cache,
    value_cache,
    new_keys,
    new_values,
    cache_lengths,
    residual,
    move_plan,
    norm_gain,
    expert_ids,
    gate_weights,
    w_gate,
    w_up,
    w_down,
):
    requests, model_width = queries.shape
    slots, width = key_cache.shape[1:]
    ep_count = lax.axis_size("ep")
    plan = move_plan.T
    cache = shape_of(key_cache.shape, BF16)
    row = shape_of((1, model_width), F32)
    moving = shape_of((2 * slots, width), BF16)
    summed_shape = shape_of((requests, model_width), F32)
    steps = distances(ep_count)

    def attend(*refs):
        attend_kernel(ep_count, *refs)

    keys, values, carry, row0, row1, cache0, cache1 = call(
        attend,
        (cache, cache, shape_of((3 * requests, model_width), F32), row, row, moving, moving),
        (cache_lengths, plan),
        (
            queries,
            key_cache,
            value_cache,
            new_keys,
            new_values,
            residual,
            expert_ids,
            norm_gain.reshape(1, model_width),
        ),
        (),
        10**8,
        3 * 10**6,
        limit=58,
    )
    got_row0 = rotate(row0, "ep", steps[0])
    got_row1 = rotate(row1, "ep", steps[1])

    def place(*refs):
        place_kernel(ep_count, *refs)

    part = model_width // COLS
    summed, outgoing = call(
        place,
        (summed_shape, shape_of((ep_count * MOST * COLS, part), BF16)),
        (),
        (),
        (carry, got_row0, got_row1),
        10**8,
        2 * 10**6,
    )
    rows = exchange(outgoing)
    cache0, cache1, rows = lax.optimization_barrier((cache0, cache1, rows))
    got_cache0 = rotate(cache0, "ep", steps[0])
    got_cache1 = rotate(cache1, "ep", steps[1])

    def settle(*refs):
        settle_kernel(ep_count, *refs)

    sums, (got_cache0, got_cache1) = through_experts(
        rows, (w_gate, w_up, w_down), (got_cache0, got_cache1)
    )
    keys_out, values_out = pl.pallas_call(
        settle,
        out_shape=(cache, cache),
        grid_spec=pltpu.PrefetchScalarGridSpec(
            num_scalar_prefetch=1,
            grid=(),
            in_specs=[VMEM, VMEM, HBM, HBM],
            out_specs=(HBM, HBM),
            scratch_shapes=[pltpu.SemaphoreType.DMA((MIG, 2))],
        ),
        input_output_aliases={3: 0, 4: 1},
        compiler_params=pltpu.CompilerParams(vmem_limit_bytes=4 * 2**20),
        cost_estimate=pl.CostEstimate(flops=0, bytes_accessed=10**6, transcendentals=0),
    )(plan, got_cache0, got_cache1, keys, values)
    returned = exchange(after(sums, keys_out, values_out))
    layer_out = call(
        mix_kernel,
        shape_of((requests, model_width), BF16),
        (),
        (expert_ids, gate_weights),
        (summed, returned),
        10**8,
        2 * 10**6,
    )
    return (layer_out, keys_out, values_out)


def solution(mesh):
    rows = P(("dp", "ep"), None)
    caches = P(("dp", "ep"), None, None)
    placed = (
        rows,
        caches,
        caches,
        rows,
        rows,
        P(("dp", "ep")),
        rows,
        rows,
        P(),
        rows,
        rows,
        P("ep", None, "dp"),
        P("ep", None, "dp"),
        P("ep", "dp", None),
    )
    return jax.shard_map(
        local,
        mesh=mesh,
        in_specs=placed,
        out_specs=(rows, caches, caches),
        check_vma=False,
    )
```

```python
import math

import jax
import jax.numpy as jnp
from jax import lax
from jax.experimental import pallas as pl
from jax.experimental.pallas import tpu as pltpu
from jax.sharding import PartitionSpec as P

HD = 128
TOP = 8
MIG = 2
MOST = 2
COLS = 8
STEP = 512
SIDE = 1536
F32 = jnp.float32
BF16 = jnp.bfloat16
VMEM = pl.BlockSpec(memory_space=pltpu.VMEM)
HBM = pl.BlockSpec(memory_space=pltpu.HBM)


def iota(shape, dim):
    return lax.broadcasted_iota(jnp.int32, shape, dim)


def one_hot(condition):
    return jnp.where(condition, 1.0, 0.0).astype(BF16)


def distances(ep_count):
    return tuple(1 + d * (ep_count // 2 - 1) for d in range(MIG))


def find_slot(plan_ref, column, rank, per_device, ep_count):
    found = jnp.int32(0)
    for r in range(per_device):
        other = lax.rem(lax.div(plan_ref[column, r], per_device), ep_count)
        found = jnp.where(other == rank, jnp.int32(r), found)
    return found


def attend_kernel(
    ep_count,
    lengths_ref,
    plan_ref,
    queries_ref,
    keys_ref,
    values_ref,
    new_keys_ref,
    new_values_ref,
    residual_ref,
    ids_ref,
    gain_ref,
    keys_out_ref,
    values_out_ref,
    carry_ref,
    row0_ref,
    row1_ref,
    cache0_ref,
    cache1_ref,
):
    requests, slots, width = keys_ref.shape
    heads = queries_ref.shape[1] // HD
    kv_heads = width // HD
    groups = heads // kv_heads
    fresh_keys = new_keys_ref[...].astype(F32)
    fresh_values = new_values_ref[...].astype(F32)
    position = iota((slots, width), 0)
    for r in range(requests):
        newest = position == lengths_ref[r]
        keys_out_ref[r] = jnp.where(
            newest, fresh_keys[r : r + 1], keys_ref[r].astype(F32)
        ).astype(BF16)
        values_out_ref[r] = jnp.where(
            newest, fresh_values[r : r + 1], values_ref[r].astype(F32)
        ).astype(BF16)
    total = requests * slots
    column = iota((groups * requests, total), 1)
    holder = lax.div(column, slots)
    limit = jnp.zeros_like(column)
    for r in range(requests):
        limit = jnp.where(holder == r, lengths_ref[r], limit)
    own_row = lax.rem(iota((groups * requests, total), 0), requests)
    visible = (holder == own_row) & (lax.rem(column, slots) <= limit)
    queries = queries_ref[...].astype(F32)
    residual = residual_ref[...].astype(F32)
    all_keys = keys_out_ref[...].reshape(total, width)
    all_values = values_out_ref[...].reshape(total, width)
    for k in range(kv_heads):
        stacked = jnp.concatenate(
            [
                queries[:, (k * groups + h) * HD : (k * groups + h + 1) * HD]
                for h in range(groups)
            ],
            axis=0,
        ).astype(BF16)
        scores = lax.dot_general(
            stacked,
            all_keys[:, k * HD : (k + 1) * HD],
            (((1,), (1,)), ((), ())),
            preferred_element_type=F32,
        ) * (1.0 / math.sqrt(HD))
        scores = jnp.where(visible, scores, -jnp.inf)
        weights = jnp.exp(scores - jnp.max(scores, axis=1, keepdims=True))
        probabilities = (weights / jnp.sum(weights, axis=1, keepdims=True)).astype(BF16)
        attended = jnp.dot(
            probabilities, all_values[:, k * HD : (k + 1) * HD], preferred_element_type=F32
        )
        for h in range(groups):
            place = slice((k * groups + h) * HD, (k * groups + h + 1) * HD)
            carry_ref[0:requests, place] = (
                residual[:, place] + attended[h * requests : (h + 1) * requests]
            )
    rank = lax.axis_index("ep")
    summed = carry_ref[0:requests]
    row_number = iota(summed.shape, 0)
    for d, (distance, row_ref, cache_ref) in enumerate(
        zip(distances(ep_count), (row0_ref, row1_ref), (cache0_ref, cache1_ref))
    ):
        slot = find_slot(plan_ref, 1, lax.rem(rank + distance, ep_count), requests, ep_count)
        row_ref[...] = jnp.sum(jnp.where(row_number == slot, summed, 0.0), axis=0, keepdims=True)
        cache_ref[0:slots] = keys_out_ref[slot]
        cache_ref[slots : 2 * slots] = values_out_ref[slot]
        origin = lax.rem(rank + ep_count - distance, ep_count)
        arrival = find_slot(plan_ref, 0, origin, requests, ep_count)
        carry_ref[2 * requests : 3 * requests, (2 + d) * HD : (3 + d) * HD] = jnp.where(
            iota((requests, HD), 0) == arrival, 1.0, 0.0
        )
    carry_ref[requests : 2 * requests] = jnp.broadcast_to(gain_ref[...], summed.shape)
    chosen, _, earlier = routes(ids_ref[...], None, ep_count)
    carry_ref[2 * requests : 3 * requests, 0:ep_count] = chosen
    carry_ref[2 * requests : 3 * requests, HD : HD + ep_count] = earlier


def routes(ids, gates, experts):
    rows = ids.shape[0]
    expert = iota((rows, experts), 1)
    chosen = jnp.zeros((rows, experts), F32)
    weight = jnp.zeros((rows, experts), F32)
    for k in range(TOP):
        same = ids[:, k : k + 1] == expert
        chosen = jnp.where(same, 1.0, chosen)
        if gates is not None:
            weight = jnp.where(same, gates[:, k : k + 1], weight)
    earlier = []
    running = jnp.zeros((1, experts), F32)
    for r in range(rows):
        earlier.append(running)
        running = running + chosen[r : r + 1]
    return chosen, weight, jnp.concatenate(earlier, axis=0)


def place_kernel(ep_count, carry_ref, row0_ref, row1_ref, summed_out_ref, slots_ref):
    rows, model_width = summed_out_ref.shape
    summed = carry_ref[0:rows]
    notes = slice(2 * rows, 3 * rows)
    for d, row_ref in enumerate((row0_ref, row1_ref)):
        arrival = carry_ref[notes, (2 + d) * HD : (2 + d) * HD + 1]
        summed = jnp.where(arrival > 0.5, row_ref[...], summed)
    summed_out_ref[...] = summed
    scale = lax.rsqrt(jnp.mean(summed * summed, axis=1, keepdims=True) + 1e-06)
    normed = summed * scale * carry_ref[rows : 2 * rows]
    part = model_width // COLS
    pieces = jnp.concatenate(
        [normed[:, c * part : (c + 1) * part] for c in range(COLS)], axis=0
    ).astype(BF16)
    chosen = carry_ref[notes, 0:ep_count]
    earlier = carry_ref[notes, HD : HD + ep_count]
    deep = MOST * COLS
    wide = (ep_count * deep, ep_count)
    spread = one_hot(lax.div(iota(wide, 0), deep) == iota(wide, 1))
    repeat_shape = (rows, COLS * rows)
    repeat = one_hot(iota(repeat_shape, 0) == lax.rem(iota(repeat_shape, 1), rows))
    pick_shape = (ep_count * deep, COLS * rows)
    row_here = iota(pick_shape, 0)
    same_part = lax.rem(row_here, COLS) == lax.div(iota(pick_shape, 1), rows)
    slot_here = lax.rem(lax.div(row_here, COLS), MOST)
    pick = jnp.zeros(pick_shape, F32)
    for s in range(MOST):
        placed = jnp.where(earlier == float(s), chosen, 0.0).astype(BF16)
        by_expert = lax.dot_general(
            placed, repeat, (((0,), (0,)), ((), ())), preferred_element_type=F32
        ).astype(BF16)
        by_piece = jnp.dot(spread, by_expert, preferred_element_type=F32)
        pick = jnp.where(same_part & (slot_here == s), by_piece, pick)
    slots_ref[...] = jnp.dot(pick.astype(BF16), pieces, preferred_element_type=F32).astype(BF16)


def regroup(rows):
    shape = (rows, rows)
    count = rows // COLS
    first = iota(shape, 0)
    return one_hot(
        iota(shape, 1) == lax.rem(first, count) * COLS + lax.div(first, count)
    )


def expert_kernel(n_pieces, n_blocks, *refs):
    piece_refs = refs[:n_pieces]
    gate_ref, up_ref, down_ref = refs[n_pieces : n_pieces + 3]
    out_refs = refs[n_pieces + 3 : n_pieces + 3 + n_blocks]
    hidden_refs = refs[n_pieces + 3 + n_blocks : -1]
    rows_ref = refs[-1]
    model_width, hidden_width = gate_ref.shape[1:]
    count = STEP // COLS
    part = model_width // COLS
    order = regroup(STEP)
    n = 0
    for ref in piece_refs:
        for m in range(ref.shape[0] // STEP):
            sorted_rows = jnp.dot(
                order, ref[m * STEP : (m + 1) * STEP], preferred_element_type=F32
            ).astype(BF16)
            for c in range(COLS):
                rows_ref[n * count : (n + 1) * count, c * part : (c + 1) * part] = sorted_rows[
                    c * count : (c + 1) * count
                ]
            n += 1
    rows = rows_ref[...]
    gate_proj = jnp.dot(rows, gate_ref[0], preferred_element_type=F32)
    up_proj = jnp.dot(rows, up_ref[0], preferred_element_type=F32)
    hidden = (gate_proj / (1.0 + jnp.exp(-gate_proj)) * up_proj).astype(BF16)
    per_group = hidden.shape[0] // len(hidden_refs)
    for i, ref in enumerate(hidden_refs):
        ref[...] = hidden[i * per_group : (i + 1) * per_group]
    for c in range((model_width - SIDE) // part):
        term = jnp.dot(
            hidden, down_ref[0, :, c * part : (c + 1) * part], preferred_element_type=F32
        ).astype(BF16)
        for n in range(n_blocks):
            out_refs[n][c * count : (c + 1) * count] = term[n * count : (n + 1) * count]


def relay_kernel(right_ref, left_ref, from_left_ref, from_right_ref, to_right_ref, to_left_ref):
    to_right_ref[...] = (right_ref[...].astype(F32) + from_left_ref[...].astype(F32)).astype(BF16)
    to_left_ref[...] = (left_ref[...].astype(F32) + from_right_ref[...].astype(F32)).astype(BF16)


def down_kernel(*refs):
    hidden_refs, (own_ref, left_ref, right_ref, top_ref, bottom_ref) = refs[:4], refs[4:9]
    out_refs = refs[9:]
    far = jnp.concatenate([top_ref[...], bottom_ref[...]], axis=0)
    matrices = (own_ref[...], left_ref[...], right_ref[...], far)
    count, part = STEP // COLS, out_refs[0].shape[1]
    total = jnp.zeros((hidden_refs[0].shape[0], far.shape[1]), F32)
    for ref, matrix in zip(hidden_refs, matrices):
        total += jnp.dot(ref[...], matrix, preferred_element_type=F32)
    total = total.astype(BF16)
    for i, out_ref in enumerate(out_refs):
        for c in range(far.shape[1] // part):
            out_ref[c * count : (c + 1) * count] = total[
                i * count : (i + 1) * count, c * part : (c + 1) * part
            ]


def gather_kernel(
    own_top_ref,
    own_bottom_ref,
    left_top_ref,
    left_bottom_ref,
    right_top_ref,
    right_bottom_ref,
    side_top_ref,
    side_bottom_ref,
    out_ref,
):
    order = regroup(STEP)
    for i, (side_ref, *refs) in enumerate(
        (
            (side_top_ref, own_top_ref, left_top_ref, right_top_ref),
            (side_bottom_ref, own_bottom_ref, left_bottom_ref, right_bottom_ref),
        )
    ):
        total = sum(ref[...].astype(F32) for ref in refs).astype(BF16)
        total = jnp.concatenate([total, side_ref[...]], axis=0)
        out_ref[i * STEP : (i + 1) * STEP] = lax.dot_general(
            order, total, (((0,), (0,)), ((), ())), preferred_element_type=F32
        ).astype(BF16)


def mix_kernel(ids_ref, gates_ref, summed_ref, returned_ref, out_ref):
    rows, model_width = summed_ref.shape
    deep = MOST * COLS
    experts = returned_ref.shape[0] // deep
    part = model_width // COLS
    chosen, weight, earlier = routes(ids_ref[...], gates_ref[...], experts)
    repeat_shape = (COLS * rows, rows)
    repeat = one_hot(lax.rem(iota(repeat_shape, 0), rows) == iota(repeat_shape, 1))
    wide = (experts, experts * deep)
    spread = one_hot(iota(wide, 0) == lax.div(iota(wide, 1), deep))
    pick_shape = (COLS * rows, experts * deep)
    column = iota(pick_shape, 1)
    same_part = lax.div(iota(pick_shape, 0), rows) == lax.rem(column, COLS)
    slot_here = lax.rem(lax.div(column, COLS), MOST)
    returned = returned_ref[...]
    coarse_pick = jnp.zeros(pick_shape, F32)
    fine_pick = jnp.zeros(pick_shape, F32)
    for s in range(MOST):
        placed = jnp.where((earlier == float(s)) & (chosen > 0.5), weight, 0.0)
        coarse = placed.astype(BF16)
        fine = (placed - coarse.astype(F32)).astype(BF16)
        here = same_part & (slot_here == s)
        by_row = jnp.dot(
            jnp.dot(repeat, coarse, preferred_element_type=F32).astype(BF16),
            spread,
            preferred_element_type=F32,
        )
        coarse_pick = jnp.where(here, by_row, coarse_pick)
        by_row = jnp.dot(
            jnp.dot(repeat, fine, preferred_element_type=F32).astype(BF16),
            spread,
            preferred_element_type=F32,
        )
        fine_pick = jnp.where(here, by_row, fine_pick)
    mixture = jnp.dot(coarse_pick.astype(BF16), returned, preferred_element_type=F32)
    mixture += jnp.dot(fine_pick.astype(BF16), returned, preferred_element_type=F32)
    for c in range(COLS):
        here = slice(c * part, (c + 1) * part)
        out_ref[:, here] = (
            summed_ref[:, here] + mixture[c * rows : (c + 1) * rows]
        ).astype(BF16)


def settle_kernel(
    ep_count,
    plan_ref,
    cache0_ref,
    cache1_ref,
    keys_in_ref,
    values_in_ref,
    keys_ref,
    values_ref,
    sems,
):
    del keys_in_ref, values_in_ref
    requests, slots, _ = keys_ref.shape
    rank = lax.axis_index("ep")
    copies = []
    for d, (distance, cache_ref) in enumerate(zip(distances(ep_count), (cache0_ref, cache1_ref))):
        origin = lax.rem(rank + ep_count - distance, ep_count)
        slot = find_slot(plan_ref, 0, origin, requests, ep_count)
        for i, ref in enumerate((keys_ref, values_ref)):
            copies.append(
                pltpu.make_async_copy(
                    cache_ref.at[pl.ds(i * slots, slots)], ref.at[slot], sems.at[d, i]
                )
            )
            copies[-1].start()
    for copy in copies:
        copy.wait()


def shape_of(shape, dtype):
    return jax.ShapeDtypeStruct(shape, dtype)


def call(kernel, outs, scalars, staged, resident, flops, moved, limit=16, scratch=()):
    n_scalars, n_staged, n_resident = map(len, (scalars, staged, resident))
    n_outs = len(outs) if isinstance(outs, tuple) else 1

    def body(*refs):
        refs = list(refs)

        def take(count):
            taken = refs[:count]
            del refs[:count]
            return taken

        scalar_refs, sources, resident_refs, out_refs = map(
            take, (n_scalars, n_staged, n_resident, n_outs)
        )
        own_refs = take(len(scratch))
        staged_refs = take(n_staged)
        copies = [
            pltpu.make_async_copy(source, target, refs[0].at[i])
            for i, (source, target) in enumerate(zip(sources, staged_refs))
        ]
        for copy in copies:
            copy.start()
        for copy in copies:
            copy.wait()
        kernel(*scalar_refs, *staged_refs, *resident_refs, *out_refs, *own_refs)

    stages = [pltpu.VMEM(arg.shape, arg.dtype) for arg in staged]
    if staged:
        stages.append(pltpu.SemaphoreType.DMA((n_staged,)))
    return pl.pallas_call(
        body,
        out_shape=outs,
        grid_spec=pltpu.PrefetchScalarGridSpec(
            num_scalar_prefetch=n_scalars,
            grid=(),
            in_specs=[HBM] * n_staged + [VMEM] * n_resident,
            out_specs=tuple([VMEM] * n_outs) if isinstance(outs, tuple) else VMEM,
            scratch_shapes=[*scratch, *stages],
        ),
        compiler_params=pltpu.CompilerParams(vmem_limit_bytes=limit * 2**20),
        cost_estimate=pl.CostEstimate(flops=flops, bytes_accessed=moved, transcendentals=0),
    )(*scalars, *staged, *resident)


def experts_of(pieces, weights):
    rows = sum(piece.shape[0] for piece in pieces)
    part = pieces[0].shape[1]
    n_blocks = rows // STEP
    model_width, hidden_width = weights[0].shape[1:]
    tokens = rows // COLS
    terms = (model_width - SIDE) // part * (STEP // COLS)

    def kernel(*refs):
        expert_kernel(len(pieces), n_blocks, *refs)

    return call(
        kernel,
        tuple(shape_of((terms, part), BF16) for _ in range(n_blocks))
        + tuple(shape_of((2 * STEP // COLS, hidden_width), BF16) for _ in range(n_blocks // 2)),
        (),
        (),
        (*pieces, *weights),
        6 * tokens * model_width * hidden_width,
        6 * model_width * hidden_width + 4 * rows * part,
        limit=20,
        scratch=[pltpu.VMEM((tokens, model_width), BF16)],
    )


def rotate(member, axis, distance):
    count = lax.axis_size(axis)
    return lax.ppermute(member, axis, [(s, (s + distance) % count) for s in range(count)])


def exchange(member):
    experts = lax.axis_size("ep")
    cut = member.reshape(experts, member.shape[0] // experts, member.shape[1])
    cut = lax.all_to_all(cut, "ep", split_axis=0, concat_axis=0, tiled=True)
    return cut.reshape(member.shape)


def after(member, *earlier):
    return lax.optimization_barrier((member, *earlier))[0]


def gather_down(w_down):
    own = w_down[0, :, w_down.shape[2] - SIDE :]
    half = own.shape[0] // 2
    from_left = rotate(own, "dp", 1)
    from_right = rotate(own, "dp", -1)
    far_top = rotate(from_left[:half], "dp", 1)
    far_bottom = rotate(from_right[half:], "dp", -1)
    return own, from_left, from_right, far_top, far_bottom


def through_experts(own, weights, side_weights, beside):
    own, *side_weights = lax.optimization_barrier((own, *side_weights))
    from_left = rotate(own, "dp", 1)
    from_right = rotate(own, "dp", -1)
    own_top, own_bottom, own_hidden = experts_of([own], weights)
    from_left, from_right, own_top, own_bottom, *beside = lax.optimization_barrier(
        (from_left, from_right, own_top, own_bottom, *beside)
    )
    far_top = rotate(from_left[:STEP], "dp", 1)
    far_bottom = rotate(from_right[STEP:], "dp", -1)
    left_top, left_bottom, right_top, right_bottom, left_hidden, right_hidden = experts_of(
        [from_left, from_right], weights
    )
    far_top, far_bottom, right_top, left_bottom = lax.optimization_barrier(
        (far_top, far_bottom, right_top, left_bottom)
    )
    direct_left = rotate(after(right_bottom, far_top, far_bottom), "dp", 1)
    direct_right = rotate(after(left_top, far_top, far_bottom), "dp", -1)
    *far_terms, far_hidden = experts_of([far_top, far_bottom], weights)
    relayed_left = rotate(far_terms[0], "dp", 1)
    relayed_right = rotate(far_terms[1], "dp", -1)
    hidden_left = rotate(after(right_hidden, far_top, far_bottom), "dp", 1)
    hidden_right = rotate(after(left_hidden, far_top, far_bottom), "dp", -1)
    hidden_far = rotate(far_hidden, "dp", 2)
    block = shape_of(far_terms[0].shape, BF16)
    size = 2 * block.size
    to_right, to_left = call(
        relay_kernel,
        (block, block),
        (),
        (),
        (right_top, left_bottom, relayed_left, relayed_right),
        size,
        5 * size,
    )
    sums_left = rotate(to_right, "dp", 1)
    sums_right = rotate(to_left, "dp", -1)
    part = block.shape[1]
    side_block = shape_of((SIDE // part * (STEP // COLS), part), BF16)
    side_top, side_bottom = call(
        down_kernel,
        (side_block, side_block),
        (),
        (),
        (own_hidden, hidden_left, hidden_right, hidden_far, *side_weights),
        10**9,
        6 * 10**6,
    )
    sums = call(
        gather_kernel,
        shape_of((2 * STEP, part), BF16),
        (),
        (),
        (
            own_top,
            own_bottom,
            sums_left,
            direct_left,
            direct_right,
            sums_right,
            side_top,
            side_bottom,
        ),
        2 * size * STEP,
        8 * size,
    )
    return sums, beside


def local(
    queries,
    key_cache,
    value_cache,
    new_keys,
    new_values,
    cache_lengths,
    residual,
    move_plan,
    norm_gain,
    expert_ids,
    gate_weights,
    w_gate,
    w_up,
    w_down,
):
    requests, model_width = queries.shape
    slots, width = key_cache.shape[1:]
    ep_count = lax.axis_size("ep")
    plan = move_plan.T
    cache = shape_of(key_cache.shape, BF16)
    row = shape_of((1, model_width), F32)
    moving = shape_of((2 * slots, width), BF16)
    summed_shape = shape_of((requests, model_width), F32)
    steps = distances(ep_count)

    side_weights = gather_down(w_down)

    def attend(*refs):
        attend_kernel(ep_count, *refs)

    keys, values, carry, row0, row1, cache0, cache1 = call(
        attend,
        (cache, cache, shape_of((3 * requests, model_width), F32), row, row, moving, moving),
        (cache_lengths, plan),
        (
            queries,
            key_cache,
            value_cache,
            new_keys,
            new_values,
            residual,
            expert_ids,
            norm_gain.reshape(1, model_width),
        ),
        (),
        10**8,
        3 * 10**6,
        limit=58,
    )
    got_row0 = rotate(row0, "ep", steps[0])
    got_row1 = rotate(row1, "ep", steps[1])

    def place(*refs):
        place_kernel(ep_count, *refs)

    part = model_width // COLS
    summed, outgoing = call(
        place,
        (summed_shape, shape_of((ep_count * MOST * COLS, part), BF16)),
        (),
        (),
        (carry, got_row0, got_row1),
        10**8,
        2 * 10**6,
    )
    rows = exchange(outgoing)
    cache0, cache1, rows = lax.optimization_barrier((cache0, cache1, rows))
    got_cache0 = rotate(cache0, "ep", steps[0])
    got_cache1 = rotate(cache1, "ep", steps[1])

    def settle(*refs):
        settle_kernel(ep_count, *refs)

    sums, (got_cache0, got_cache1) = through_experts(
        rows, (w_gate, w_up, w_down), side_weights, (got_cache0, got_cache1)
    )
    keys_out, values_out = pl.pallas_call(
        settle,
        out_shape=(cache, cache),
        grid_spec=pltpu.PrefetchScalarGridSpec(
            num_scalar_prefetch=1,
            grid=(),
            in_specs=[VMEM, VMEM, HBM, HBM],
            out_specs=(HBM, HBM),
            scratch_shapes=[pltpu.SemaphoreType.DMA((MIG, 2))],
        ),
        input_output_aliases={3: 0, 4: 1},
        compiler_params=pltpu.CompilerParams(vmem_limit_bytes=4 * 2**20),
        cost_estimate=pl.CostEstimate(flops=0, bytes_accessed=10**6, transcendentals=0),
    )(plan, got_cache0, got_cache1, keys, values)
    returned = exchange(after(sums, keys_out, values_out))
    layer_out = call(
        mix_kernel,
        shape_of((requests, model_width), BF16),
        (),
        (expert_ids, gate_weights),
        (summed, returned),
        10**8,
        2 * 10**6,
    )
    return (layer_out, keys_out, values_out)


def solution(mesh):
    rows = P(("dp", "ep"), None)
    caches = P(("dp", "ep"), None, None)
    placed = (
        rows,
        caches,
        caches,
        rows,
        rows,
        P(("dp", "ep")),
        rows,
        rows,
        P(),
        rows,
        rows,
        P("ep", None, "dp"),
        P("ep", None, "dp"),
        P("ep", "dp", None),
    )
    return jax.shard_map(
        local,
        mesh=mesh,
        in_specs=placed,
        out_specs=(rows, caches, caches),
        check_vma=False,
    )
```

```python
import math

import jax
import jax.numpy as jnp
from jax import lax
from jax.experimental import pallas as pl
from jax.experimental.pallas import tpu as pltpu
from jax.sharding import PartitionSpec as P

HD = 128
TOP = 8
MIG = 2
MOST = 2
COLS = 8
STEP = 512
F32 = jnp.float32
BF16 = jnp.bfloat16
VMEM = pl.BlockSpec(memory_space=pltpu.VMEM)
HBM = pl.BlockSpec(memory_space=pltpu.HBM)


def iota(shape, dim):
    return lax.broadcasted_iota(jnp.int32, shape, dim)


def one_hot(condition):
    return jnp.where(condition, 1.0, 0.0).astype(BF16)


def distances(ep_count):
    return tuple(1 + d * (ep_count // 2 - 1) for d in range(MIG))


def find_slot(plan_ref, column, rank, per_device, ep_count):
    found = jnp.int32(0)
    for r in range(per_device):
        other = lax.rem(lax.div(plan_ref[column, r], per_device), ep_count)
        found = jnp.where(other == rank, jnp.int32(r), found)
    return found


def insert_new(lengths_ref, cached_ref, fresh_ref, out_ref):
    requests, slots, width = cached_ref.shape
    fresh = fresh_ref[...].astype(F32)
    position = iota((slots, width), 0)
    for r in range(requests):
        out_ref[r] = jnp.where(
            position == lengths_ref[r], fresh[r : r + 1], cached_ref[r].astype(F32)
        ).astype(BF16)


def store_kernel(
    ep_count,
    lengths_ref,
    plan_ref,
    keys_ref,
    values_ref,
    new_keys_ref,
    new_values_ref,
    keys_out_ref,
    values_out_ref,
    cache0_ref,
    cache1_ref,
):
    requests, slots, _ = keys_ref.shape
    insert_new(lengths_ref, keys_ref, new_keys_ref, keys_out_ref)
    insert_new(lengths_ref, values_ref, new_values_ref, values_out_ref)
    rank = lax.axis_index("ep")
    for distance, cache_ref in zip(distances(ep_count), (cache0_ref, cache1_ref)):
        slot = find_slot(plan_ref, 1, lax.rem(rank + distance, ep_count), requests, ep_count)
        cache_ref[0:slots] = keys_out_ref[slot]
        cache_ref[slots : 2 * slots] = values_out_ref[slot]


def attend_kernel(
    ep_count,
    copies,
    lengths_ref,
    plan_ref,
    queries_ref,
    keys_ref,
    new_keys_ref,
    values_ref,
    new_values_ref,
    residual_ref,
    ids_ref,
    gain_ref,
    carry_ref,
    row0_ref,
    row1_ref,
    keys_out_ref,
    values_out_ref,
):
    requests, slots, width = keys_ref.shape
    heads = queries_ref.shape[1] // HD
    kv_heads = width // HD
    groups = heads // kv_heads
    total = requests * slots
    column = iota((groups * requests, total), 1)
    holder = lax.div(column, slots)
    limit = jnp.zeros_like(column)
    for r in range(requests):
        limit = jnp.where(holder == r, lengths_ref[r], limit)
    own_row = lax.rem(iota((groups * requests, total), 0), requests)
    visible = (holder == own_row) & (lax.rem(column, slots) <= limit)
    for copy in copies[:3]:
        copy.wait()
    insert_new(lengths_ref, keys_ref, new_keys_ref, keys_out_ref)
    queries = queries_ref[...].astype(F32)
    all_keys = keys_out_ref[...].reshape(total, width)
    spread = []
    for k in range(kv_heads):
        stacked = jnp.concatenate(
            [
                queries[:, (k * groups + h) * HD : (k * groups + h + 1) * HD]
                for h in range(groups)
            ],
            axis=0,
        ).astype(BF16)
        scores = lax.dot_general(
            stacked,
            all_keys[:, k * HD : (k + 1) * HD],
            (((1,), (1,)), ((), ())),
            preferred_element_type=F32,
        ) * (1.0 / math.sqrt(HD))
        scores = jnp.where(visible, scores, -jnp.inf)
        weights = jnp.exp(scores - jnp.max(scores, axis=1, keepdims=True))
        spread.append((weights / jnp.sum(weights, axis=1, keepdims=True)).astype(BF16))
    for copy in copies[3:]:
        copy.wait()
    insert_new(lengths_ref, values_ref, new_values_ref, values_out_ref)
    all_values = values_out_ref[...].reshape(total, width)
    residual = residual_ref[...].astype(F32)
    for k, probabilities in enumerate(spread):
        attended = jnp.dot(
            probabilities, all_values[:, k * HD : (k + 1) * HD], preferred_element_type=F32
        )
        for h in range(groups):
            place = slice((k * groups + h) * HD, (k * groups + h + 1) * HD)
            carry_ref[0:requests, place] = (
                residual[:, place] + attended[h * requests : (h + 1) * requests]
            )
    rank = lax.axis_index("ep")
    summed = carry_ref[0:requests]
    row_number = iota(summed.shape, 0)
    for d, (distance, row_ref) in enumerate(zip(distances(ep_count), (row0_ref, row1_ref))):
        slot = find_slot(plan_ref, 1, lax.rem(rank + distance, ep_count), requests, ep_count)
        row_ref[...] = jnp.sum(jnp.where(row_number == slot, summed, 0.0), axis=0, keepdims=True)
        origin = lax.rem(rank + ep_count - distance, ep_count)
        arrival = find_slot(plan_ref, 0, origin, requests, ep_count)
        carry_ref[2 * requests : 3 * requests, (2 + d) * HD : (3 + d) * HD] = jnp.where(
            iota((requests, HD), 0) == arrival, 1.0, 0.0
        )
    carry_ref[requests : 2 * requests] = jnp.broadcast_to(gain_ref[...], summed.shape)
    chosen, _, earlier = routes(ids_ref[...], None, ep_count)
    carry_ref[2 * requests : 3 * requests, 0:ep_count] = chosen
    carry_ref[2 * requests : 3 * requests, HD : HD + ep_count] = earlier


def routes(ids, gates, experts):
    rows = ids.shape[0]
    expert = iota((rows, experts), 1)
    chosen = jnp.zeros((rows, experts), F32)
    weight = jnp.zeros((rows, experts), F32)
    for k in range(TOP):
        same = ids[:, k : k + 1] == expert
        chosen = jnp.where(same, 1.0, chosen)
        if gates is not None:
            weight = jnp.where(same, gates[:, k : k + 1], weight)
    earlier = []
    running = jnp.zeros((1, experts), F32)
    for r in range(rows):
        earlier.append(running)
        running = running + chosen[r : r + 1]
    return chosen, weight, jnp.concatenate(earlier, axis=0)


def place_kernel(ep_count, carry_ref, row0_ref, row1_ref, summed_out_ref, slots_ref):
    rows, model_width = summed_out_ref.shape
    summed = carry_ref[0:rows]
    notes = slice(2 * rows, 3 * rows)
    for d, row_ref in enumerate((row0_ref, row1_ref)):
        arrival = carry_ref[notes, (2 + d) * HD : (2 + d) * HD + 1]
        summed = jnp.where(arrival > 0.5, row_ref[...], summed)
    summed_out_ref[...] = summed
    scale = lax.rsqrt(jnp.mean(summed * summed, axis=1, keepdims=True) + 1e-06)
    normed = summed * scale * carry_ref[rows : 2 * rows]
    part = model_width // COLS
    pieces = jnp.concatenate(
        [normed[:, c * part : (c + 1) * part] for c in range(COLS)], axis=0
    ).astype(BF16)
    chosen = carry_ref[notes, 0:ep_count]
    earlier = carry_ref[notes, HD : HD + ep_count]
    deep = MOST * COLS
    wide = (ep_count * deep, ep_count)
    spread = one_hot(lax.div(iota(wide, 0), deep) == iota(wide, 1))
    repeat_shape = (rows, COLS * rows)
    repeat = one_hot(iota(repeat_shape, 0) == lax.rem(iota(repeat_shape, 1), rows))
    pick_shape = (ep_count * deep, COLS * rows)
    row_here = iota(pick_shape, 0)
    same_part = lax.rem(row_here, COLS) == lax.div(iota(pick_shape, 1), rows)
    slot_here = lax.rem(lax.div(row_here, COLS), MOST)
    pick = jnp.zeros(pick_shape, F32)
    for s in range(MOST):
        placed = jnp.where(earlier == float(s), chosen, 0.0).astype(BF16)
        by_expert = lax.dot_general(
            placed, repeat, (((0,), (0,)), ((), ())), preferred_element_type=F32
        ).astype(BF16)
        by_piece = jnp.dot(spread, by_expert, preferred_element_type=F32)
        pick = jnp.where(same_part & (slot_here == s), by_piece, pick)
    slots_ref[...] = jnp.dot(pick.astype(BF16), pieces, preferred_element_type=F32).astype(BF16)


def regroup(rows):
    shape = (rows, rows)
    count = rows // COLS
    first = iota(shape, 0)
    return one_hot(
        iota(shape, 1) == lax.rem(first, count) * COLS + lax.div(first, count)
    )


def expert_kernel(n_pieces, n_blocks, *refs):
    piece_refs = refs[:n_pieces]
    gate_ref, up_ref, down_ref = refs[n_pieces : n_pieces + 3]
    out_refs = refs[n_pieces + 3 : n_pieces + 3 + n_blocks]
    rows_ref = refs[-1]
    model_width, hidden_width = gate_ref.shape[1:]
    count = STEP // COLS
    part = model_width // COLS
    order = regroup(STEP)
    n = 0
    for ref in piece_refs:
        for m in range(ref.shape[0] // STEP):
            sorted_rows = jnp.dot(
                order, ref[m * STEP : (m + 1) * STEP], preferred_element_type=F32
            ).astype(BF16)
            for c in range(COLS):
                rows_ref[n * count : (n + 1) * count, c * part : (c + 1) * part] = sorted_rows[
                    c * count : (c + 1) * count
                ]
            n += 1
    rows = rows_ref[...]
    gate_proj = jnp.dot(rows, gate_ref[0], preferred_element_type=F32)
    up_proj = jnp.dot(rows, up_ref[0], preferred_element_type=F32)
    hidden = (gate_proj / (1.0 + jnp.exp(-gate_proj)) * up_proj).astype(BF16)
    for c in range(COLS):
        term = jnp.dot(
            hidden, down_ref[0, :, c * part : (c + 1) * part], preferred_element_type=F32
        ).astype(BF16)
        for n in range(n_blocks):
            out_refs[n][c * count : (c + 1) * count] = term[n * count : (n + 1) * count]


def relay_kernel(right_ref, left_ref, from_left_ref, from_right_ref, to_right_ref, to_left_ref):
    to_right_ref[...] = (right_ref[...].astype(F32) + from_left_ref[...].astype(F32)).astype(BF16)
    to_left_ref[...] = (left_ref[...].astype(F32) + from_right_ref[...].astype(F32)).astype(BF16)


def gather_kernel(
    own_top_ref,
    own_bottom_ref,
    left_top_ref,
    left_bottom_ref,
    right_top_ref,
    right_bottom_ref,
    out_ref,
):
    order = regroup(STEP)
    for i, refs in enumerate(
        (
            (own_top_ref, left_top_ref, right_top_ref),
            (own_bottom_ref, left_bottom_ref, right_bottom_ref),
        )
    ):
        total = sum(ref[...].astype(F32) for ref in refs).astype(BF16)
        out_ref[i * STEP : (i + 1) * STEP] = lax.dot_general(
            order, total, (((0,), (0,)), ((), ())), preferred_element_type=F32
        ).astype(BF16)


def weigh_kernel(ids_ref, gates_ref, coarse_ref, fine_ref):
    rows, deep = ids_ref.shape[0], MOST * COLS
    experts = coarse_ref.shape[1] // deep
    chosen, weight, earlier = routes(ids_ref[...], gates_ref[...], experts)
    repeat_shape = (COLS * rows, rows)
    repeat = one_hot(lax.rem(iota(repeat_shape, 0), rows) == iota(repeat_shape, 1))
    wide = (experts, experts * deep)
    spread = one_hot(iota(wide, 0) == lax.div(iota(wide, 1), deep))
    pick_shape = (COLS * rows, experts * deep)
    column = iota(pick_shape, 1)
    same_part = lax.div(iota(pick_shape, 0), rows) == lax.rem(column, COLS)
    slot_here = lax.rem(lax.div(column, COLS), MOST)
    picks = [jnp.zeros(pick_shape, F32), jnp.zeros(pick_shape, F32)]
    for s in range(MOST):
        placed = jnp.where((earlier == float(s)) & (chosen > 0.5), weight, 0.0)
        coarse = placed.astype(BF16)
        fine = (placed - coarse.astype(F32)).astype(BF16)
        for i, member in enumerate((coarse, fine)):
            by_row = jnp.dot(
                jnp.dot(repeat, member, preferred_element_type=F32).astype(BF16),
                spread,
                preferred_element_type=F32,
            )
            picks[i] = jnp.where(same_part & (slot_here == s), by_row, picks[i])
    coarse_ref[...] = picks[0].astype(BF16)
    fine_ref[...] = picks[1].astype(BF16)


def mix_kernel(coarse_ref, fine_ref, summed_ref, returned_ref, out_ref):
    rows, model_width = summed_ref.shape
    part = model_width // COLS
    returned = returned_ref[...]
    mixture = jnp.dot(coarse_ref[...], returned, preferred_element_type=F32)
    mixture += jnp.dot(fine_ref[...], returned, preferred_element_type=F32)
    for c in range(COLS):
        here = slice(c * part, (c + 1) * part)
        out_ref[:, here] = (
            summed_ref[:, here] + mixture[c * rows : (c + 1) * rows]
        ).astype(BF16)


def settle_kernel(
    ep_count,
    plan_ref,
    cache0_ref,
    cache1_ref,
    keys_in_ref,
    values_in_ref,
    keys_ref,
    values_ref,
    sems,
):
    del keys_in_ref, values_in_ref
    requests, slots, _ = keys_ref.shape
    rank = lax.axis_index("ep")
    copies = []
    for d, (distance, cache_ref) in enumerate(zip(distances(ep_count), (cache0_ref, cache1_ref))):
        origin = lax.rem(rank + ep_count - distance, ep_count)
        slot = find_slot(plan_ref, 0, origin, requests, ep_count)
        for i, ref in enumerate((keys_ref, values_ref)):
            copies.append(
                pltpu.make_async_copy(
                    cache_ref.at[pl.ds(i * slots, slots)], ref.at[slot], sems.at[d, i]
                )
            )
            copies[-1].start()
    for copy in copies:
        copy.wait()


def shape_of(shape, dtype):
    return jax.ShapeDtypeStruct(shape, dtype)


def call(kernel, outs, scalars, staged, resident, flops, moved, limit=16, scratch=(), lazy=False):
    n_scalars, n_staged, n_resident = map(len, (scalars, staged, resident))
    n_outs = len(outs) if isinstance(outs, tuple) else 1

    def body(*refs):
        refs = list(refs)

        def take(count):
            taken = refs[:count]
            del refs[:count]
            return taken

        scalar_refs, sources, resident_refs, out_refs = map(
            take, (n_scalars, n_staged, n_resident, n_outs)
        )
        own_refs = take(len(scratch))
        staged_refs = take(n_staged)
        copies = [
            pltpu.make_async_copy(source, target, refs[0].at[i])
            for i, (source, target) in enumerate(zip(sources, staged_refs))
        ]
        for copy in copies:
            copy.start()
        if not lazy:
            for copy in copies:
                copy.wait()
        first = (copies,) if lazy else ()
        kernel(*first, *scalar_refs, *staged_refs, *resident_refs, *out_refs, *own_refs)

    stages = [pltpu.VMEM(arg.shape, arg.dtype) for arg in staged]
    if staged:
        stages.append(pltpu.SemaphoreType.DMA((n_staged,)))
    return pl.pallas_call(
        body,
        out_shape=outs,
        grid_spec=pltpu.PrefetchScalarGridSpec(
            num_scalar_prefetch=n_scalars,
            grid=(),
            in_specs=[HBM] * n_staged + [VMEM] * n_resident,
            out_specs=tuple([VMEM] * n_outs) if isinstance(outs, tuple) else VMEM,
            scratch_shapes=[*scratch, *stages],
        ),
        compiler_params=pltpu.CompilerParams(vmem_limit_bytes=limit * 2**20),
        cost_estimate=pl.CostEstimate(flops=flops, bytes_accessed=moved, transcendentals=0),
    )(*scalars, *staged, *resident)


def experts_of(pieces, weights):
    rows = sum(piece.shape[0] for piece in pieces)
    part = pieces[0].shape[1]
    n_blocks = rows // STEP
    model_width, hidden_width = weights[0].shape[1:]
    tokens = rows // COLS

    def kernel(*refs):
        expert_kernel(len(pieces), n_blocks, *refs)

    return call(
        kernel,
        tuple(shape_of((STEP, part), BF16) for _ in range(n_blocks)),
        (),
        (),
        (*pieces, *weights),
        6 * tokens * model_width * hidden_width,
        6 * model_width * hidden_width + 4 * rows * part,
        limit=20,
        scratch=[pltpu.VMEM((tokens, model_width), BF16)],
    )


def rotate(member, axis, distance):
    count = lax.axis_size(axis)
    return lax.ppermute(member, axis, [(s, (s + distance) % count) for s in range(count)])


def exchange(member):
    experts = lax.axis_size("ep")
    cut = member.reshape(experts, member.shape[0] // experts, member.shape[1])
    cut = lax.all_to_all(cut, "ep", split_axis=0, concat_axis=0, tiled=True)
    return cut.reshape(member.shape)


def after(member, *earlier):
    return lax.optimization_barrier((member, *earlier))[0]


def through_experts(own, weights, beside):
    top, bottom = own[:STEP], own[STEP:]
    left_rows_top = rotate(top, "dp", 1)
    right_rows_bottom = rotate(bottom, "dp", -1)
    left_rows_bottom = rotate(bottom, "dp", 1)
    right_rows_top = rotate(top, "dp", -1)
    own_top, own_bottom = experts_of([own], weights)
    left_rows_top, right_rows_bottom, own_top, own_bottom, beside = lax.optimization_barrier(
        (left_rows_top, right_rows_bottom, own_top, own_bottom, beside)
    )
    far_top = rotate(left_rows_top, "dp", 1)
    far_bottom = rotate(right_rows_bottom, "dp", -1)
    left_top, left_bottom, right_top, right_bottom = experts_of(
        [left_rows_top, left_rows_bottom, right_rows_top, right_rows_bottom], weights
    )
    direct_left = rotate(right_bottom, "dp", 1)
    direct_right = rotate(left_top, "dp", -1)
    far_top, far_bottom, right_top, left_bottom = lax.optimization_barrier(
        (far_top, far_bottom, right_top, left_bottom)
    )
    far_terms = experts_of([far_top, far_bottom], weights)
    relayed_left = rotate(far_terms[0], "dp", 1)
    relayed_right = rotate(far_terms[1], "dp", -1)
    block = shape_of(far_top.shape, BF16)
    size = 2 * block.size
    to_right, to_left = call(
        relay_kernel,
        (block, block),
        (),
        (),
        (right_top, left_bottom, relayed_left, relayed_right),
        size,
        5 * size,
    )
    sums_left = rotate(to_right, "dp", 1)
    sums_right = rotate(to_left, "dp", -1)
    sums = call(
        gather_kernel,
        shape_of(own.shape, BF16),
        (),
        (),
        (own_top, own_bottom, sums_left, direct_left, direct_right, sums_right),
        2 * size * STEP,
        8 * size,
    )
    return sums, beside


def local(
    queries,
    key_cache,
    value_cache,
    new_keys,
    new_values,
    cache_lengths,
    residual,
    move_plan,
    norm_gain,
    expert_ids,
    gate_weights,
    w_gate,
    w_up,
    w_down,
):
    requests, model_width = queries.shape
    slots, width = key_cache.shape[1:]
    ep_count = lax.axis_size("ep")
    plan = move_plan.T
    cache = shape_of(key_cache.shape, BF16)
    row = shape_of((1, model_width), F32)
    moving = shape_of((2 * slots, width), BF16)
    summed_shape = shape_of((requests, model_width), F32)
    steps = distances(ep_count)

    def attend(*refs):
        attend_kernel(ep_count, *refs)

    carry, row0, row1 = call(
        attend,
        (shape_of((3 * requests, model_width), F32), row, row),
        (cache_lengths, plan),
        (
            queries,
            key_cache,
            new_keys,
            value_cache,
            new_values,
            residual,
            expert_ids,
            norm_gain.reshape(1, model_width),
        ),
        (),
        10**8,
        3 * 10**6,
        limit=58,
        lazy=True,
        scratch=[pltpu.VMEM(cache.shape, BF16), pltpu.VMEM(cache.shape, BF16)],
    )
    got_row0 = rotate(row0, "ep", steps[0])
    got_row1 = rotate(row1, "ep", steps[1])

    def place(*refs):
        place_kernel(ep_count, *refs)

    part = model_width // COLS
    summed, outgoing = call(
        place,
        (summed_shape, shape_of((ep_count * MOST * COLS, part), BF16)),
        (),
        (),
        (carry, got_row0, got_row1),
        10**8,
        2 * 10**6,
    )
    rows = exchange(outgoing)

    def store(*refs):
        store_kernel(ep_count, *refs)

    keys, values, cache0, cache1 = call(
        store,
        (cache, cache, moving, moving),
        (cache_lengths, plan),
        (after(key_cache, rows), value_cache, new_keys, new_values),
        (),
        0,
        3 * 10**6,
    )
    got_cache0 = rotate(cache0, "ep", steps[0])
    got_cache1 = rotate(cache1, "ep", steps[1])

    def settle(*refs):
        settle_kernel(ep_count, *refs)

    sums, got_cache0 = through_experts(rows, (w_gate, w_up, w_down), got_cache0)
    keys_out, values_out = pl.pallas_call(
        settle,
        out_shape=(cache, cache),
        grid_spec=pltpu.PrefetchScalarGridSpec(
            num_scalar_prefetch=1,
            grid=(),
            in_specs=[VMEM, VMEM, HBM, HBM],
            out_specs=(HBM, HBM),
            scratch_shapes=[pltpu.SemaphoreType.DMA((MIG, 2))],
        ),
        input_output_aliases={3: 0, 4: 1},
        compiler_params=pltpu.CompilerParams(vmem_limit_bytes=4 * 2**20),
        cost_estimate=pl.CostEstimate(flops=0, bytes_accessed=10**6, transcendentals=0),
    )(plan, got_cache0, got_cache1, keys, values)
    picks = shape_of((COLS * requests, ep_count * MOST * COLS), BF16)
    coarse, fine = call(
        weigh_kernel,
        (picks, picks),
        (),
        (),
        (after(expert_ids, rows), gate_weights),
        10**7,
        10**6,
    )
    returned = exchange(after(sums, keys_out, values_out, coarse, fine))
    layer_out = call(
        mix_kernel,
        shape_of((requests, model_width), BF16),
        (),
        (),
        (coarse, fine, summed, returned),
        10**8,
        2 * 10**6,
    )
    return (layer_out, keys_out, values_out)


def solution(mesh):
    rows = P(("dp", "ep"), None)
    caches = P(("dp", "ep"), None, None)
    placed = (
        rows,
        caches,
        caches,
        rows,
        rows,
        P(("dp", "ep")),
        rows,
        rows,
        P(),
        rows,
        rows,
        P("ep", None, "dp"),
        P("ep", None, "dp"),
        P("ep", "dp", None),
    )
    return jax.shard_map(
        local,
        mesh=mesh,
        in_specs=placed,
        out_specs=(rows, caches, caches),
        check_vma=False,
    )
```

```python
import math

import jax
import jax.numpy as jnp
from jax import lax
from jax.experimental import pallas as pl
from jax.experimental.pallas import tpu as pltpu
from jax.sharding import PartitionSpec as P

HD = 128
TOP = 8
MIG = 2
MOST = 2
COLS = 8
STEP = 512
F32 = jnp.float32
BF16 = jnp.bfloat16
VMEM = pl.BlockSpec(memory_space=pltpu.VMEM)
HBM = pl.BlockSpec(memory_space=pltpu.HBM)


def iota(shape, dim):
    return lax.broadcasted_iota(jnp.int32, shape, dim)


def one_hot(condition):
    return jnp.where(condition, 1.0, 0.0).astype(BF16)


def distances(ep_count):
    return tuple(1 + d * (ep_count // 2 - 1) for d in range(MIG))


def find_slot(plan_ref, column, rank, per_device, ep_count):
    found = jnp.int32(0)
    for r in range(per_device):
        other = lax.rem(lax.div(plan_ref[column, r], per_device), ep_count)
        found = jnp.where(other == rank, jnp.int32(r), found)
    return found


def insert_new(lengths_ref, cached_ref, fresh_ref, out_ref):
    requests, slots, width = cached_ref.shape
    fresh = fresh_ref[...].astype(F32)
    position = iota((slots, width), 0)
    for r in range(requests):
        out_ref[r] = jnp.where(
            position == lengths_ref[r], fresh[r : r + 1], cached_ref[r].astype(F32)
        ).astype(BF16)


def store_kernel(
    ep_count,
    lengths_ref,
    plan_ref,
    keys_ref,
    values_ref,
    new_keys_ref,
    new_values_ref,
    keys_out_ref,
    values_out_ref,
    cache0_ref,
    cache1_ref,
):
    requests, slots, _ = keys_ref.shape
    insert_new(lengths_ref, keys_ref, new_keys_ref, keys_out_ref)
    insert_new(lengths_ref, values_ref, new_values_ref, values_out_ref)
    rank = lax.axis_index("ep")
    for distance, cache_ref in zip(distances(ep_count), (cache0_ref, cache1_ref)):
        slot = find_slot(plan_ref, 1, lax.rem(rank + distance, ep_count), requests, ep_count)
        cache_ref[0:slots] = keys_out_ref[slot]
        cache_ref[slots : 2 * slots] = values_out_ref[slot]


def attend_kernel(
    ep_count,
    copies,
    lengths_ref,
    plan_ref,
    queries_ref,
    keys_ref,
    new_keys_ref,
    values_ref,
    new_values_ref,
    residual_ref,
    ids_ref,
    gain_ref,
    carry_ref,
    row0_ref,
    row1_ref,
    keys_out_ref,
    values_out_ref,
):
    requests, slots, width = keys_ref.shape
    heads = queries_ref.shape[1] // HD
    kv_heads = width // HD
    groups = heads // kv_heads
    total = requests * slots
    column = iota((groups * requests, total), 1)
    holder = lax.div(column, slots)
    limit = jnp.zeros_like(column)
    for r in range(requests):
        limit = jnp.where(holder == r, lengths_ref[r], limit)
    own_row = lax.rem(iota((groups * requests, total), 0), requests)
    visible = (holder == own_row) & (lax.rem(column, slots) <= limit)
    for copy in copies[:3]:
        copy.wait()
    insert_new(lengths_ref, keys_ref, new_keys_ref, keys_out_ref)
    queries = queries_ref[...].astype(F32)
    all_keys = keys_out_ref[...].reshape(total, width)
    spread = []
    for k in range(kv_heads):
        stacked = jnp.concatenate(
            [
                queries[:, (k * groups + h) * HD : (k * groups + h + 1) * HD]
                for h in range(groups)
            ],
            axis=0,
        ).astype(BF16)
        scores = lax.dot_general(
            stacked,
            all_keys[:, k * HD : (k + 1) * HD],
            (((1,), (1,)), ((), ())),
            preferred_element_type=F32,
        ) * (1.0 / math.sqrt(HD))
        scores = jnp.where(visible, scores, -jnp.inf)
        weights = jnp.exp(scores - jnp.max(scores, axis=1, keepdims=True))
        spread.append((weights / jnp.sum(weights, axis=1, keepdims=True)).astype(BF16))
    for copy in copies[3:]:
        copy.wait()
    insert_new(lengths_ref, values_ref, new_values_ref, values_out_ref)
    all_values = values_out_ref[...].reshape(total, width)
    residual = residual_ref[...].astype(F32)
    for k, probabilities in enumerate(spread):
        attended = jnp.dot(
            probabilities, all_values[:, k * HD : (k + 1) * HD], preferred_element_type=F32
        )
        for h in range(groups):
            place = slice((k * groups + h) * HD, (k * groups + h + 1) * HD)
            carry_ref[0:requests, place] = (
                residual[:, place] + attended[h * requests : (h + 1) * requests]
            )
    rank = lax.axis_index("ep")
    summed = carry_ref[0:requests]
    row_number = iota(summed.shape, 0)
    for d, (distance, row_ref) in enumerate(zip(distances(ep_count), (row0_ref, row1_ref))):
        slot = find_slot(plan_ref, 1, lax.rem(rank + distance, ep_count), requests, ep_count)
        row_ref[...] = jnp.sum(jnp.where(row_number == slot, summed, 0.0), axis=0, keepdims=True)
        origin = lax.rem(rank + ep_count - distance, ep_count)
        arrival = find_slot(plan_ref, 0, origin, requests, ep_count)
        carry_ref[2 * requests : 3 * requests, (2 + d) * HD : (3 + d) * HD] = jnp.where(
            iota((requests, HD), 0) == arrival, 1.0, 0.0
        )
    carry_ref[requests : 2 * requests] = jnp.broadcast_to(gain_ref[...], summed.shape)
    chosen, _, earlier = routes(ids_ref[...], None, ep_count)
    carry_ref[2 * requests : 3 * requests, 0:ep_count] = chosen
    carry_ref[2 * requests : 3 * requests, HD : HD + ep_count] = earlier


def routes(ids, gates, experts):
    rows = ids.shape[0]
    expert = iota((rows, experts), 1)
    chosen = jnp.zeros((rows, experts), F32)
    weight = jnp.zeros((rows, experts), F32)
    for k in range(TOP):
        same = ids[:, k : k + 1] == expert
        chosen = jnp.where(same, 1.0, chosen)
        if gates is not None:
            weight = jnp.where(same, gates[:, k : k + 1], weight)
    earlier = []
    running = jnp.zeros((1, experts), F32)
    for r in range(rows):
        earlier.append(running)
        running = running + chosen[r : r + 1]
    return chosen, weight, jnp.concatenate(earlier, axis=0)


def place_kernel(ep_count, carry_ref, row0_ref, row1_ref, summed_out_ref, slots_ref):
    rows, model_width = summed_out_ref.shape
    summed = carry_ref[0:rows]
    notes = slice(2 * rows, 3 * rows)
    for d, row_ref in enumerate((row0_ref, row1_ref)):
        arrival = carry_ref[notes, (2 + d) * HD : (2 + d) * HD + 1]
        summed = jnp.where(arrival > 0.5, row_ref[...], summed)
    summed_out_ref[...] = summed
    scale = lax.rsqrt(jnp.mean(summed * summed, axis=1, keepdims=True) + 1e-06)
    normed = summed * scale * carry_ref[rows : 2 * rows]
    part = model_width // COLS
    pieces = jnp.concatenate(
        [normed[:, c * part : (c + 1) * part] for c in range(COLS)], axis=0
    ).astype(BF16)
    chosen = carry_ref[notes, 0:ep_count]
    earlier = carry_ref[notes, HD : HD + ep_count]
    deep = MOST * COLS
    wide = (ep_count * deep, ep_count)
    spread = one_hot(lax.div(iota(wide, 0), deep) == iota(wide, 1))
    repeat_shape = (rows, COLS * rows)
    repeat = one_hot(iota(repeat_shape, 0) == lax.rem(iota(repeat_shape, 1), rows))
    pick_shape = (ep_count * deep, COLS * rows)
    row_here = iota(pick_shape, 0)
    same_part = lax.rem(row_here, COLS) == lax.div(iota(pick_shape, 1), rows)
    slot_here = lax.rem(lax.div(row_here, COLS), MOST)
    pick = jnp.zeros(pick_shape, F32)
    for s in range(MOST):
        placed = jnp.where(earlier == float(s), chosen, 0.0).astype(BF16)
        by_expert = lax.dot_general(
            placed, repeat, (((0,), (0,)), ((), ())), preferred_element_type=F32
        ).astype(BF16)
        by_piece = jnp.dot(spread, by_expert, preferred_element_type=F32)
        pick = jnp.where(same_part & (slot_here == s), by_piece, pick)
    slots_ref[...] = jnp.dot(pick.astype(BF16), pieces, preferred_element_type=F32).astype(BF16)


def regroup(rows):
    shape = (rows, rows)
    count = rows // COLS
    first = iota(shape, 0)
    return one_hot(
        iota(shape, 1) == lax.rem(first, count) * COLS + lax.div(first, count)
    )


def expert_kernel(n_pieces, n_blocks, *refs):
    piece_refs = refs[:n_pieces]
    gate_ref, up_ref, down_ref = refs[n_pieces : n_pieces + 3]
    out_refs = refs[n_pieces + 3 : n_pieces + 3 + n_blocks]
    rows_ref = refs[-1]
    model_width, hidden_width = gate_ref.shape[1:]
    count = STEP // COLS
    part = model_width // COLS
    order = regroup(STEP)
    n = 0
    for ref in piece_refs:
        for m in range(ref.shape[0] // STEP):
            sorted_rows = jnp.dot(
                order, ref[m * STEP : (m + 1) * STEP], preferred_element_type=F32
            ).astype(BF16)
            for c in range(COLS):
                rows_ref[n * count : (n + 1) * count, c * part : (c + 1) * part] = sorted_rows[
                    c * count : (c + 1) * count
                ]
            n += 1
    rows = rows_ref[...]
    gate_proj = jnp.dot(rows, gate_ref[0], preferred_element_type=F32)
    up_proj = jnp.dot(rows, up_ref[0], preferred_element_type=F32)
    hidden = (gate_proj / (1.0 + jnp.exp(-gate_proj)) * up_proj).astype(BF16)
    for c in range(COLS):
        term = jnp.dot(
            hidden, down_ref[0, :, c * part : (c + 1) * part], preferred_element_type=F32
        ).astype(BF16)
        for n in range(n_blocks):
            out_refs[n][c * count : (c + 1) * count] = term[n * count : (n + 1) * count]


def relay_kernel(right_ref, left_ref, from_left_ref, from_right_ref, to_right_ref, to_left_ref):
    to_right_ref[...] = (right_ref[...].astype(F32) + from_left_ref[...].astype(F32)).astype(BF16)
    to_left_ref[...] = (left_ref[...].astype(F32) + from_right_ref[...].astype(F32)).astype(BF16)


def gather_kernel(
    own_top_ref,
    own_bottom_ref,
    left_top_ref,
    left_bottom_ref,
    right_top_ref,
    right_bottom_ref,
    out_ref,
):
    order = regroup(STEP)
    for i, refs in enumerate(
        (
            (own_top_ref, left_top_ref, right_top_ref),
            (own_bottom_ref, left_bottom_ref, right_bottom_ref),
        )
    ):
        total = sum(ref[...].astype(F32) for ref in refs).astype(BF16)
        out_ref[i * STEP : (i + 1) * STEP] = lax.dot_general(
            order, total, (((0,), (0,)), ((), ())), preferred_element_type=F32
        ).astype(BF16)


def weigh_kernel(ids_ref, gates_ref, coarse_ref, fine_ref):
    rows, deep = ids_ref.shape[0], MOST * COLS
    experts = coarse_ref.shape[1] // deep
    chosen, weight, earlier = routes(ids_ref[...], gates_ref[...], experts)
    repeat_shape = (COLS * rows, rows)
    repeat = one_hot(lax.rem(iota(repeat_shape, 0), rows) == iota(repeat_shape, 1))
    wide = (experts, experts * deep)
    spread = one_hot(iota(wide, 0) == lax.div(iota(wide, 1), deep))
    pick_shape = (COLS * rows, experts * deep)
    column = iota(pick_shape, 1)
    same_part = lax.div(iota(pick_shape, 0), rows) == lax.rem(column, COLS)
    slot_here = lax.rem(lax.div(column, COLS), MOST)
    picks = [jnp.zeros(pick_shape, F32), jnp.zeros(pick_shape, F32)]
    for s in range(MOST):
        placed = jnp.where((earlier == float(s)) & (chosen > 0.5), weight, 0.0)
        coarse = placed.astype(BF16)
        fine = (placed - coarse.astype(F32)).astype(BF16)
        for i, member in enumerate((coarse, fine)):
            by_row = jnp.dot(
                jnp.dot(repeat, member, preferred_element_type=F32).astype(BF16),
                spread,
                preferred_element_type=F32,
            )
            picks[i] = jnp.where(same_part & (slot_here == s), by_row, picks[i])
    coarse_ref[...] = picks[0].astype(BF16)
    fine_ref[...] = picks[1].astype(BF16)


def mix_kernel(coarse_ref, fine_ref, summed_ref, returned_ref, out_ref):
    rows, model_width = summed_ref.shape
    part = model_width // COLS
    returned = returned_ref[...]
    mixture = jnp.dot(coarse_ref[...], returned, preferred_element_type=F32)
    mixture += jnp.dot(fine_ref[...], returned, preferred_element_type=F32)
    for c in range(COLS):
        here = slice(c * part, (c + 1) * part)
        out_ref[:, here] = (
            summed_ref[:, here] + mixture[c * rows : (c + 1) * rows]
        ).astype(BF16)


def settle_kernel(
    ep_count,
    plan_ref,
    cache0_ref,
    cache1_ref,
    keys_in_ref,
    values_in_ref,
    keys_ref,
    values_ref,
    sems,
):
    del keys_in_ref, values_in_ref
    requests, slots, _ = keys_ref.shape
    rank = lax.axis_index("ep")
    copies = []
    for d, (distance, cache_ref) in enumerate(zip(distances(ep_count), (cache0_ref, cache1_ref))):
        origin = lax.rem(rank + ep_count - distance, ep_count)
        slot = find_slot(plan_ref, 0, origin, requests, ep_count)
        for i, ref in enumerate((keys_ref, values_ref)):
            copies.append(
                pltpu.make_async_copy(
                    cache_ref.at[pl.ds(i * slots, slots)], ref.at[slot], sems.at[d, i]
                )
            )
            copies[-1].start()
    for copy in copies:
        copy.wait()


def shape_of(shape, dtype):
    return jax.ShapeDtypeStruct(shape, dtype)


def call(kernel, outs, scalars, staged, resident, flops, moved, limit=16, scratch=(), lazy=False):
    n_scalars, n_staged, n_resident = map(len, (scalars, staged, resident))
    n_outs = len(outs) if isinstance(outs, tuple) else 1

    def body(*refs):
        refs = list(refs)

        def take(count):
            taken = refs[:count]
            del refs[:count]
            return taken

        scalar_refs, sources, resident_refs, out_refs = map(
            take, (n_scalars, n_staged, n_resident, n_outs)
        )
        own_refs = take(len(scratch))
        staged_refs = take(n_staged)
        copies = [
            pltpu.make_async_copy(source, target, refs[0].at[i])
            for i, (source, target) in enumerate(zip(sources, staged_refs))
        ]
        for copy in copies:
            copy.start()
        if not lazy:
            for copy in copies:
                copy.wait()
        first = (copies,) if lazy else ()
        kernel(*first, *scalar_refs, *staged_refs, *resident_refs, *out_refs, *own_refs)

    stages = [pltpu.VMEM(arg.shape, arg.dtype) for arg in staged]
    if staged:
        stages.append(pltpu.SemaphoreType.DMA((n_staged,)))
    return pl.pallas_call(
        body,
        out_shape=outs,
        grid_spec=pltpu.PrefetchScalarGridSpec(
            num_scalar_prefetch=n_scalars,
            grid=(),
            in_specs=[HBM] * n_staged + [VMEM] * n_resident,
            out_specs=tuple([VMEM] * n_outs) if isinstance(outs, tuple) else VMEM,
            scratch_shapes=[*scratch, *stages],
        ),
        compiler_params=pltpu.CompilerParams(vmem_limit_bytes=limit * 2**20),
        cost_estimate=pl.CostEstimate(flops=flops, bytes_accessed=moved, transcendentals=0),
    )(*scalars, *staged, *resident)


def experts_of(pieces, weights):
    rows = sum(piece.shape[0] for piece in pieces)
    part = pieces[0].shape[1]
    n_blocks = rows // STEP
    model_width, hidden_width = weights[0].shape[1:]
    tokens = rows // COLS

    def kernel(*refs):
        expert_kernel(len(pieces), n_blocks, *refs)

    return call(
        kernel,
        tuple(shape_of((STEP, part), BF16) for _ in range(n_blocks)),
        (),
        (),
        (*pieces, *weights),
        6 * tokens * model_width * hidden_width,
        6 * model_width * hidden_width + 4 * rows * part,
        limit=20,
        scratch=[pltpu.VMEM((tokens, model_width), BF16)],
    )


def rotate(member, axis, distance):
    count = lax.axis_size(axis)
    return lax.ppermute(member, axis, [(s, (s + distance) % count) for s in range(count)])


def exchange(member):
    experts = lax.axis_size("ep")
    cut = member.reshape(experts, member.shape[0] // experts, member.shape[1])
    cut = lax.all_to_all(cut, "ep", split_axis=0, concat_axis=0, tiled=True)
    return cut.reshape(member.shape)


def after(member, *earlier):
    return lax.optimization_barrier((member, *earlier))[0]


def through_experts(own, weights, beside):
    top, bottom = own[:STEP], own[STEP:]
    left_rows_top = rotate(top, "dp", 1)
    right_rows_bottom = rotate(bottom, "dp", -1)
    left_rows_bottom = rotate(bottom, "dp", 1)
    right_rows_top = rotate(top, "dp", -1)
    own_top, own_bottom = experts_of([own], weights)
    left_rows_top, right_rows_bottom, own_top, own_bottom, beside = lax.optimization_barrier(
        (left_rows_top, right_rows_bottom, own_top, own_bottom, beside)
    )
    far_top = rotate(left_rows_top, "dp", 1)
    far_bottom = rotate(right_rows_bottom, "dp", -1)
    left_top, left_bottom, right_top, right_bottom = experts_of(
        [left_rows_top, left_rows_bottom, right_rows_top, right_rows_bottom], weights
    )
    direct_left = rotate(right_bottom, "dp", 1)
    direct_right = rotate(left_top, "dp", -1)
    far_top, far_bottom, right_top, left_bottom = lax.optimization_barrier(
        (far_top, far_bottom, right_top, left_bottom)
    )
    far_terms = experts_of([far_top, far_bottom], weights)
    relayed_left = rotate(far_terms[0], "dp", 1)
    relayed_right = rotate(far_terms[1], "dp", -1)
    relayed_left, relayed_right, direct_left, direct_right = lax.optimization_barrier(
        (relayed_left, relayed_right, direct_left, direct_right)
    )
    block = shape_of(far_top.shape, BF16)
    size = 2 * block.size
    to_right, to_left = call(
        relay_kernel,
        (block, block),
        (),
        (),
        (right_top, left_bottom, relayed_left, relayed_right),
        size,
        5 * size,
    )
    sums_left = rotate(to_right, "dp", 1)
    sums_right = rotate(to_left, "dp", -1)
    sums = call(
        gather_kernel,
        shape_of(own.shape, BF16),
        (),
        (),
        (own_top, own_bottom, sums_left, direct_left, direct_right, sums_right),
        2 * size * STEP,
        8 * size,
    )
    return sums, beside


def local(
    queries,
    key_cache,
    value_cache,
    new_keys,
    new_values,
    cache_lengths,
    residual,
    move_plan,
    norm_gain,
    expert_ids,
    gate_weights,
    w_gate,
    w_up,
    w_down,
):
    requests, model_width = queries.shape
    slots, width = key_cache.shape[1:]
    ep_count = lax.axis_size("ep")
    plan = move_plan.T
    cache = shape_of(key_cache.shape, BF16)
    row = shape_of((1, model_width), F32)
    moving = shape_of((2 * slots, width), BF16)
    summed_shape = shape_of((requests, model_width), F32)
    steps = distances(ep_count)

    def attend(*refs):
        attend_kernel(ep_count, *refs)

    carry, row0, row1 = call(
        attend,
        (shape_of((3 * requests, model_width), F32), row, row),
        (cache_lengths, plan),
        (
            queries,
            key_cache,
            new_keys,
            value_cache,
            new_values,
            residual,
            expert_ids,
            norm_gain.reshape(1, model_width),
        ),
        (),
        10**8,
        3 * 10**6,
        limit=58,
        lazy=True,
        scratch=[pltpu.VMEM(cache.shape, BF16), pltpu.VMEM(cache.shape, BF16)],
    )
    got_row0 = rotate(row0, "ep", steps[0])
    got_row1 = rotate(row1, "ep", steps[1])

    def place(*refs):
        place_kernel(ep_count, *refs)

    part = model_width // COLS
    summed, outgoing = call(
        place,
        (summed_shape, shape_of((ep_count * MOST * COLS, part), BF16)),
        (),
        (),
        (carry, got_row0, got_row1),
        10**8,
        2 * 10**6,
    )
    rows = exchange(outgoing)

    def store(*refs):
        store_kernel(ep_count, *refs)

    keys, values, cache0, cache1 = call(
        store,
        (cache, cache, moving, moving),
        (cache_lengths, plan),
        (after(key_cache, rows), value_cache, new_keys, new_values),
        (),
        0,
        3 * 10**6,
    )
    got_cache0 = rotate(cache0, "ep", steps[0])
    got_cache1 = rotate(cache1, "ep", steps[1])

    def settle(*refs):
        settle_kernel(ep_count, *refs)

    sums, got_cache0 = through_experts(rows, (w_gate, w_up, w_down), got_cache0)
    keys_out, values_out = pl.pallas_call(
        settle,
        out_shape=(cache, cache),
        grid_spec=pltpu.PrefetchScalarGridSpec(
            num_scalar_prefetch=1,
            grid=(),
            in_specs=[VMEM, VMEM, HBM, HBM],
            out_specs=(HBM, HBM),
            scratch_shapes=[pltpu.SemaphoreType.DMA((MIG, 2))],
        ),
        input_output_aliases={3: 0, 4: 1},
        compiler_params=pltpu.CompilerParams(vmem_limit_bytes=4 * 2**20),
        cost_estimate=pl.CostEstimate(flops=0, bytes_accessed=10**6, transcendentals=0),
    )(plan, got_cache0, got_cache1, keys, values)
    picks = shape_of((COLS * requests, ep_count * MOST * COLS), BF16)
    coarse, fine = call(
        weigh_kernel,
        (picks, picks),
        (),
        (),
        (after(expert_ids, rows), gate_weights),
        10**7,
        10**6,
    )
    returned = exchange(after(sums, keys_out, values_out, coarse, fine))
    layer_out = call(
        mix_kernel,
        shape_of((requests, model_width), BF16),
        (),
        (),
        (coarse, fine, summed, returned),
        10**8,
        2 * 10**6,
    )
    return (layer_out, keys_out, values_out)


def solution(mesh):
    rows = P(("dp", "ep"), None)
    caches = P(("dp", "ep"), None, None)
    placed = (
        rows,
        caches,
        caches,
        rows,
        rows,
        P(("dp", "ep")),
        rows,
        rows,
        P(),
        rows,
        rows,
        P("ep", None, "dp"),
        P("ep", None, "dp"),
        P("ep", "dp", None),
    )
    return jax.shard_map(
        local,
        mesh=mesh,
        in_specs=placed,
        out_specs=(rows, caches, caches),
        check_vma=False,
    )
```

```python
import math

import jax
import jax.numpy as jnp
from jax import lax
from jax.experimental import pallas as pl
from jax.experimental.pallas import tpu as pltpu
from jax.sharding import PartitionSpec as P

HD = 128
TOP = 8
MIG = 2
MOST = 2
COLS = 8
STEP = 512
F32 = jnp.float32
BF16 = jnp.bfloat16
VMEM = pl.BlockSpec(memory_space=pltpu.VMEM)
HBM = pl.BlockSpec(memory_space=pltpu.HBM)


def iota(shape, dim):
    return lax.broadcasted_iota(jnp.int32, shape, dim)


def one_hot(condition):
    return jnp.where(condition, 1.0, 0.0).astype(BF16)


def distances(ep_count):
    return tuple(1 + d * (ep_count // 2 - 1) for d in range(MIG))


def find_slot(plan_ref, column, rank, per_device, ep_count):
    found = jnp.int32(0)
    for r in range(per_device):
        other = lax.rem(lax.div(plan_ref[column, r], per_device), ep_count)
        found = jnp.where(other == rank, jnp.int32(r), found)
    return found


def insert_new(lengths_ref, cached_ref, fresh_ref, out_ref):
    requests, slots, width = cached_ref.shape
    fresh = fresh_ref[...].astype(F32)
    position = iota((slots, width), 0)
    for r in range(requests):
        out_ref[r] = jnp.where(
            position == lengths_ref[r], fresh[r : r + 1], cached_ref[r].astype(F32)
        ).astype(BF16)


def store_kernel(
    ep_count,
    lengths_ref,
    plan_ref,
    keys_ref,
    values_ref,
    new_keys_ref,
    new_values_ref,
    keys_out_ref,
    values_out_ref,
    cache0_ref,
    cache1_ref,
):
    requests, slots, _ = keys_ref.shape
    insert_new(lengths_ref, keys_ref, new_keys_ref, keys_out_ref)
    insert_new(lengths_ref, values_ref, new_values_ref, values_out_ref)
    rank = lax.axis_index("ep")
    for distance, cache_ref in zip(distances(ep_count), (cache0_ref, cache1_ref)):
        slot = find_slot(plan_ref, 1, lax.rem(rank + distance, ep_count), requests, ep_count)
        cache_ref[0:slots] = keys_out_ref[slot]
        cache_ref[slots : 2 * slots] = values_out_ref[slot]


def attend_kernel(
    ep_count,
    copies,
    lengths_ref,
    plan_ref,
    queries_ref,
    keys_ref,
    new_keys_ref,
    values_ref,
    new_values_ref,
    residual_ref,
    ids_ref,
    gain_ref,
    carry_ref,
    row0_ref,
    row1_ref,
    keys_out_ref,
    values_out_ref,
):
    requests, slots, width = keys_ref.shape
    heads = queries_ref.shape[1] // HD
    kv_heads = width // HD
    groups = heads // kv_heads
    total = requests * slots
    column = iota((groups * requests, total), 1)
    holder = lax.div(column, slots)
    limit = jnp.zeros_like(column)
    for r in range(requests):
        limit = jnp.where(holder == r, lengths_ref[r], limit)
    own_row = lax.rem(iota((groups * requests, total), 0), requests)
    visible = (holder == own_row) & (lax.rem(column, slots) <= limit)
    for copy in copies[:3]:
        copy.wait()
    insert_new(lengths_ref, keys_ref, new_keys_ref, keys_out_ref)
    queries = queries_ref[...].astype(F32)
    all_keys = keys_out_ref[...].reshape(total, width)
    spread = []
    for k in range(kv_heads):
        stacked = jnp.concatenate(
            [
                queries[:, (k * groups + h) * HD : (k * groups + h + 1) * HD]
                for h in range(groups)
            ],
            axis=0,
        ).astype(BF16)
        scores = lax.dot_general(
            stacked,
            all_keys[:, k * HD : (k + 1) * HD],
            (((1,), (1,)), ((), ())),
            preferred_element_type=F32,
        ) * (1.0 / math.sqrt(HD))
        scores = jnp.where(visible, scores, -jnp.inf)
        weights = jnp.exp(scores - jnp.max(scores, axis=1, keepdims=True))
        spread.append((weights / jnp.sum(weights, axis=1, keepdims=True)).astype(BF16))
    for copy in copies[3:]:
        copy.wait()
    insert_new(lengths_ref, values_ref, new_values_ref, values_out_ref)
    all_values = values_out_ref[...].reshape(total, width)
    residual = residual_ref[...].astype(F32)
    for k, probabilities in enumerate(spread):
        attended = jnp.dot(
            probabilities, all_values[:, k * HD : (k + 1) * HD], preferred_element_type=F32
        )
        for h in range(groups):
            place = slice((k * groups + h) * HD, (k * groups + h + 1) * HD)
            carry_ref[0:requests, place] = (
                residual[:, place] + attended[h * requests : (h + 1) * requests]
            )
    rank = lax.axis_index("ep")
    summed = carry_ref[0:requests]
    row_number = iota(summed.shape, 0)
    for d, (distance, row_ref) in enumerate(zip(distances(ep_count), (row0_ref, row1_ref))):
        slot = find_slot(plan_ref, 1, lax.rem(rank + distance, ep_count), requests, ep_count)
        row_ref[...] = jnp.sum(jnp.where(row_number == slot, summed, 0.0), axis=0, keepdims=True)
        origin = lax.rem(rank + ep_count - distance, ep_count)
        arrival = find_slot(plan_ref, 0, origin, requests, ep_count)
        carry_ref[2 * requests : 3 * requests, (2 + d) * HD : (3 + d) * HD] = jnp.where(
            iota((requests, HD), 0) == arrival, 1.0, 0.0
        )
    carry_ref[requests : 2 * requests] = jnp.broadcast_to(gain_ref[...], summed.shape)
    chosen, _, earlier = routes(ids_ref[...], None, ep_count)
    carry_ref[2 * requests : 3 * requests, 0:ep_count] = chosen
    carry_ref[2 * requests : 3 * requests, HD : HD + ep_count] = earlier


def routes(ids, gates, experts):
    rows = ids.shape[0]
    expert = iota((rows, experts), 1)
    chosen = jnp.zeros((rows, experts), F32)
    weight = jnp.zeros((rows, experts), F32)
    for k in range(TOP):
        same = ids[:, k : k + 1] == expert
        chosen = jnp.where(same, 1.0, chosen)
        if gates is not None:
            weight = jnp.where(same, gates[:, k : k + 1], weight)
    earlier = []
    running = jnp.zeros((1, experts), F32)
    for r in range(rows):
        earlier.append(running)
        running = running + chosen[r : r + 1]
    return chosen, weight, jnp.concatenate(earlier, axis=0)


def place_kernel(ep_count, carry_ref, row0_ref, row1_ref, summed_out_ref, slots_ref):
    rows, model_width = summed_out_ref.shape
    summed = carry_ref[0:rows]
    notes = slice(2 * rows, 3 * rows)
    for d, row_ref in enumerate((row0_ref, row1_ref)):
        arrival = carry_ref[notes, (2 + d) * HD : (2 + d) * HD + 1]
        summed = jnp.where(arrival > 0.5, row_ref[...], summed)
    summed_out_ref[...] = summed
    scale = lax.rsqrt(jnp.mean(summed * summed, axis=1, keepdims=True) + 1e-06)
    normed = summed * scale * carry_ref[rows : 2 * rows]
    part = model_width // COLS
    pieces = jnp.concatenate(
        [normed[:, c * part : (c + 1) * part] for c in range(COLS)], axis=0
    ).astype(BF16)
    chosen = carry_ref[notes, 0:ep_count]
    earlier = carry_ref[notes, HD : HD + ep_count]
    deep = MOST * COLS
    wide = (ep_count * deep, ep_count)
    spread = one_hot(lax.div(iota(wide, 0), deep) == iota(wide, 1))
    repeat_shape = (rows, COLS * rows)
    repeat = one_hot(iota(repeat_shape, 0) == lax.rem(iota(repeat_shape, 1), rows))
    pick_shape = (ep_count * deep, COLS * rows)
    row_here = iota(pick_shape, 0)
    same_part = lax.rem(row_here, COLS) == lax.div(iota(pick_shape, 1), rows)
    slot_here = lax.rem(lax.div(row_here, COLS), MOST)
    pick = jnp.zeros(pick_shape, F32)
    for s in range(MOST):
        placed = jnp.where(earlier == float(s), chosen, 0.0).astype(BF16)
        by_expert = lax.dot_general(
            placed, repeat, (((0,), (0,)), ((), ())), preferred_element_type=F32
        ).astype(BF16)
        by_piece = jnp.dot(spread, by_expert, preferred_element_type=F32)
        pick = jnp.where(same_part & (slot_here == s), by_piece, pick)
    slots_ref[...] = jnp.dot(pick.astype(BF16), pieces, preferred_element_type=F32).astype(BF16)


def regroup(rows):
    shape = (rows, rows)
    count = rows // COLS
    first = iota(shape, 0)
    return one_hot(
        iota(shape, 1) == lax.rem(first, count) * COLS + lax.div(first, count)
    )


def expert_kernel(n_pieces, n_blocks, cuts, *refs):
    piece_refs = refs[:n_pieces]
    gate_ref, up_ref, down_ref = refs[n_pieces : n_pieces + 3]
    out_refs = refs[n_pieces + 3 : n_pieces + 3 + cuts * n_blocks]
    rows_ref = refs[-1]
    model_width, hidden_width = gate_ref.shape[1:]
    count = STEP // COLS
    part = model_width // COLS
    order = regroup(STEP)
    n = 0
    for ref in piece_refs:
        for m in range(ref.shape[0] // STEP):
            sorted_rows = jnp.dot(
                order, ref[m * STEP : (m + 1) * STEP], preferred_element_type=F32
            ).astype(BF16)
            for c in range(COLS):
                rows_ref[n * count : (n + 1) * count, c * part : (c + 1) * part] = sorted_rows[
                    c * count : (c + 1) * count
                ]
            n += 1
    rows = rows_ref[...]
    gate_proj = jnp.dot(rows, gate_ref[0], preferred_element_type=F32)
    up_proj = jnp.dot(rows, up_ref[0], preferred_element_type=F32)
    hidden = (gate_proj / (1.0 + jnp.exp(-gate_proj)) * up_proj).astype(BF16)
    for c in range(COLS):
        term = jnp.dot(
            hidden, down_ref[0, :, c * part : (c + 1) * part], preferred_element_type=F32
        ).astype(BF16)
        cut, at = divmod(c, COLS // cuts)
        for n in range(n_blocks):
            out_refs[cuts * n + cut][at * count : (at + 1) * count] = term[
                n * count : (n + 1) * count
            ]


def relay_kernel(
    cut, right_ref, left_ref, from_left_ref, from_right_ref, to_right_ref, to_left_ref
):
    rows = from_left_ref.shape[0]
    here = slice(cut * rows, (cut + 1) * rows)
    to_right_ref[...] = (right_ref[here].astype(F32) + from_left_ref[...].astype(F32)).astype(BF16)
    to_left_ref[...] = (left_ref[here].astype(F32) + from_right_ref[...].astype(F32)).astype(BF16)


def gather_kernel(
    own_top_ref,
    own_bottom_ref,
    left_bottom_ref,
    right_top_ref,
    left_first_ref,
    left_second_ref,
    right_first_ref,
    right_second_ref,
    out_ref,
):
    order = regroup(STEP)
    for i, (refs, halves) in enumerate(
        (
            ((own_top_ref, right_top_ref), (left_first_ref, left_second_ref)),
            ((own_bottom_ref, left_bottom_ref), (right_first_ref, right_second_ref)),
        )
    ):
        total = sum(ref[...].astype(F32) for ref in refs)
        total += jnp.concatenate([ref[...].astype(F32) for ref in halves], axis=0)
        out_ref[i * STEP : (i + 1) * STEP] = lax.dot_general(
            order, total.astype(BF16), (((0,), (0,)), ((), ())), preferred_element_type=F32
        ).astype(BF16)


def weigh_kernel(ids_ref, gates_ref, coarse_ref, fine_ref):
    rows, deep = ids_ref.shape[0], MOST * COLS
    experts = coarse_ref.shape[1] // deep
    chosen, weight, earlier = routes(ids_ref[...], gates_ref[...], experts)
    repeat_shape = (COLS * rows, rows)
    repeat = one_hot(lax.rem(iota(repeat_shape, 0), rows) == iota(repeat_shape, 1))
    wide = (experts, experts * deep)
    spread = one_hot(iota(wide, 0) == lax.div(iota(wide, 1), deep))
    pick_shape = (COLS * rows, experts * deep)
    column = iota(pick_shape, 1)
    same_part = lax.div(iota(pick_shape, 0), rows) == lax.rem(column, COLS)
    slot_here = lax.rem(lax.div(column, COLS), MOST)
    picks = [jnp.zeros(pick_shape, F32), jnp.zeros(pick_shape, F32)]
    for s in range(MOST):
        placed = jnp.where((earlier == float(s)) & (chosen > 0.5), weight, 0.0)
        coarse = placed.astype(BF16)
        fine = (placed - coarse.astype(F32)).astype(BF16)
        for i, member in enumerate((coarse, fine)):
            by_row = jnp.dot(
                jnp.dot(repeat, member, preferred_element_type=F32).astype(BF16),
                spread,
                preferred_element_type=F32,
            )
            picks[i] = jnp.where(same_part & (slot_here == s), by_row, picks[i])
    coarse_ref[...] = picks[0].astype(BF16)
    fine_ref[...] = picks[1].astype(BF16)


def mix_kernel(coarse_ref, fine_ref, summed_ref, returned_ref, out_ref):
    rows, model_width = summed_ref.shape
    part = model_width // COLS
    returned = returned_ref[...]
    mixture = jnp.dot(coarse_ref[...], returned, preferred_element_type=F32)
    mixture += jnp.dot(fine_ref[...], returned, preferred_element_type=F32)
    for c in range(COLS):
        here = slice(c * part, (c + 1) * part)
        out_ref[:, here] = (
            summed_ref[:, here] + mixture[c * rows : (c + 1) * rows]
        ).astype(BF16)


def settle_kernel(
    ep_count,
    plan_ref,
    cache0_ref,
    cache1_ref,
    keys_in_ref,
    values_in_ref,
    keys_ref,
    values_ref,
    sems,
):
    del keys_in_ref, values_in_ref
    requests, slots, _ = keys_ref.shape
    rank = lax.axis_index("ep")
    copies = []
    for d, (distance, cache_ref) in enumerate(zip(distances(ep_count), (cache0_ref, cache1_ref))):
        origin = lax.rem(rank + ep_count - distance, ep_count)
        slot = find_slot(plan_ref, 0, origin, requests, ep_count)
        for i, ref in enumerate((keys_ref, values_ref)):
            copies.append(
                pltpu.make_async_copy(
                    cache_ref.at[pl.ds(i * slots, slots)], ref.at[slot], sems.at[d, i]
                )
            )
            copies[-1].start()
    for copy in copies:
        copy.wait()


def shape_of(shape, dtype):
    return jax.ShapeDtypeStruct(shape, dtype)


def call(kernel, outs, scalars, staged, resident, flops, moved, limit=16, scratch=(), lazy=False):
    n_scalars, n_staged, n_resident = map(len, (scalars, staged, resident))
    n_outs = len(outs) if isinstance(outs, tuple) else 1

    def body(*refs):
        refs = list(refs)

        def take(count):
            taken = refs[:count]
            del refs[:count]
            return taken

        scalar_refs, sources, resident_refs, out_refs = map(
            take, (n_scalars, n_staged, n_resident, n_outs)
        )
        own_refs = take(len(scratch))
        staged_refs = take(n_staged)
        copies = [
            pltpu.make_async_copy(source, target, refs[0].at[i])
            for i, (source, target) in enumerate(zip(sources, staged_refs))
        ]
        for copy in copies:
            copy.start()
        if not lazy:
            for copy in copies:
                copy.wait()
        first = (copies,) if lazy else ()
        kernel(*first, *scalar_refs, *staged_refs, *resident_refs, *out_refs, *own_refs)

    stages = [pltpu.VMEM(arg.shape, arg.dtype) for arg in staged]
    if staged:
        stages.append(pltpu.SemaphoreType.DMA((n_staged,)))
    return pl.pallas_call(
        body,
        out_shape=outs,
        grid_spec=pltpu.PrefetchScalarGridSpec(
            num_scalar_prefetch=n_scalars,
            grid=(),
            in_specs=[HBM] * n_staged + [VMEM] * n_resident,
            out_specs=tuple([VMEM] * n_outs) if isinstance(outs, tuple) else VMEM,
            scratch_shapes=[*scratch, *stages],
        ),
        compiler_params=pltpu.CompilerParams(vmem_limit_bytes=limit * 2**20),
        cost_estimate=pl.CostEstimate(flops=flops, bytes_accessed=moved, transcendentals=0),
    )(*scalars, *staged, *resident)


def experts_of(pieces, weights, cuts=1):
    rows = sum(piece.shape[0] for piece in pieces)
    part = pieces[0].shape[1]
    n_blocks = rows // STEP
    model_width, hidden_width = weights[0].shape[1:]
    tokens = rows // COLS

    def kernel(*refs):
        expert_kernel(len(pieces), n_blocks, cuts, *refs)

    return call(
        kernel,
        tuple(shape_of((STEP // cuts, part), BF16) for _ in range(cuts * n_blocks)),
        (),
        (),
        (*pieces, *weights),
        6 * tokens * model_width * hidden_width,
        6 * model_width * hidden_width + 4 * rows * part,
        limit=20,
        scratch=[pltpu.VMEM((tokens, model_width), BF16)],
    )


def rotate(member, axis, distance):
    count = lax.axis_size(axis)
    return lax.ppermute(member, axis, [(s, (s + distance) % count) for s in range(count)])


def exchange(member):
    experts = lax.axis_size("ep")
    cut = member.reshape(experts, member.shape[0] // experts, member.shape[1])
    cut = lax.all_to_all(cut, "ep", split_axis=0, concat_axis=0, tiled=True)
    return cut.reshape(member.shape)


def after(member, *earlier):
    return lax.optimization_barrier((member, *earlier))[0]


def through_experts(own, weights, beside):
    top, bottom = own[:STEP], own[STEP:]
    left_rows_top = rotate(top, "dp", 1)
    right_rows_bottom = rotate(bottom, "dp", -1)
    left_rows_bottom = rotate(bottom, "dp", 1)
    right_rows_top = rotate(top, "dp", -1)
    own_top, own_bottom = experts_of([own], weights)
    one, other, distance = beside
    left_rows_top, right_rows_bottom, own_top, own_bottom, one, other = lax.optimization_barrier(
        (left_rows_top, right_rows_bottom, own_top, own_bottom, one, other)
    )
    other = rotate(other, "ep", distance)
    far_top = rotate(left_rows_top, "dp", 1)
    far_bottom = rotate(right_rows_bottom, "dp", -1)
    left_rows_bottom, right_rows_top, other = lax.optimization_barrier(
        (left_rows_bottom, right_rows_top, other)
    )
    left_top, left_bottom, right_top, right_bottom = experts_of(
        [left_rows_top, left_rows_bottom, right_rows_top, right_rows_bottom], weights
    )
    direct_left = rotate(right_bottom, "dp", 1)
    direct_right = rotate(left_top, "dp", -1)
    far_top, far_bottom, right_top, left_bottom = lax.optimization_barrier(
        (far_top, far_bottom, right_top, left_bottom)
    )
    far_terms = experts_of([far_top, far_bottom], weights, cuts=2)
    size = 2 * right_top.size
    part = right_top.shape[1]
    block = shape_of((STEP // 2, part), BF16)
    sums_left, sums_right = [], []
    to_right, to_left = direct_left, direct_right
    for cut in range(2):
        relayed_left = rotate(far_terms[cut], "dp", 1)
        relayed_right = rotate(far_terms[2 + cut], "dp", -1)
        if cut:
            sums_left.append(rotate(to_right, "dp", 1))
            sums_right.append(rotate(to_left, "dp", -1))
        relayed_left, relayed_right, *_ = lax.optimization_barrier(
            (relayed_left, relayed_right, to_right, to_left)
        )

        def relay(*refs, cut=cut):
            relay_kernel(cut, *refs)

        to_right, to_left = call(
            relay,
            (block, block),
            (),
            (),
            (right_top, left_bottom, relayed_left, relayed_right),
            size,
            5 * size,
        )
    sums_left.append(rotate(to_right, "dp", 1))
    sums_right.append(rotate(to_left, "dp", -1))
    sums = call(
        gather_kernel,
        shape_of((2 * STEP, part), BF16),
        (),
        (),
        (own_top, own_bottom, direct_left, direct_right, *sums_left, *sums_right),
        2 * size * STEP,
        8 * size,
    )
    return sums, one, other


def local(
    queries,
    key_cache,
    value_cache,
    new_keys,
    new_values,
    cache_lengths,
    residual,
    move_plan,
    norm_gain,
    expert_ids,
    gate_weights,
    w_gate,
    w_up,
    w_down,
):
    requests, model_width = queries.shape
    slots, width = key_cache.shape[1:]
    ep_count = lax.axis_size("ep")
    plan = move_plan.T
    cache = shape_of(key_cache.shape, BF16)
    row = shape_of((1, model_width), F32)
    moving = shape_of((2 * slots, width), BF16)
    summed_shape = shape_of((requests, model_width), F32)
    steps = distances(ep_count)

    def attend(*refs):
        attend_kernel(ep_count, *refs)

    carry, row0, row1 = call(
        attend,
        (shape_of((3 * requests, model_width), F32), row, row),
        (cache_lengths, plan),
        (
            queries,
            key_cache,
            new_keys,
            value_cache,
            new_values,
            residual,
            expert_ids,
            norm_gain.reshape(1, model_width),
        ),
        (),
        10**8,
        3 * 10**6,
        limit=58,
        lazy=True,
        scratch=[pltpu.VMEM(cache.shape, BF16), pltpu.VMEM(cache.shape, BF16)],
    )
    got_row0 = rotate(row0, "ep", steps[0])
    got_row1 = rotate(row1, "ep", steps[1])

    def place(*refs):
        place_kernel(ep_count, *refs)

    part = model_width // COLS
    summed, outgoing = call(
        place,
        (summed_shape, shape_of((ep_count * MOST * COLS, part), BF16)),
        (),
        (),
        (carry, got_row0, got_row1),
        10**8,
        2 * 10**6,
    )
    rows = exchange(outgoing)

    def store(*refs):
        store_kernel(ep_count, *refs)

    keys, values, cache0, cache1 = call(
        store,
        (cache, cache, moving, moving),
        (cache_lengths, plan),
        (after(key_cache, rows), value_cache, new_keys, new_values),
        (),
        0,
        3 * 10**6,
    )
    got_cache0 = rotate(cache0, "ep", steps[0])

    def settle(*refs):
        settle_kernel(ep_count, *refs)

    sums, got_cache0, got_cache1 = through_experts(
        rows, (w_gate, w_up, w_down), (got_cache0, cache1, steps[1])
    )
    keys_out, values_out = pl.pallas_call(
        settle,
        out_shape=(cache, cache),
        grid_spec=pltpu.PrefetchScalarGridSpec(
            num_scalar_prefetch=1,
            grid=(),
            in_specs=[VMEM, VMEM, HBM, HBM],
            out_specs=(HBM, HBM),
            scratch_shapes=[pltpu.SemaphoreType.DMA((MIG, 2))],
        ),
        input_output_aliases={3: 0, 4: 1},
        compiler_params=pltpu.CompilerParams(vmem_limit_bytes=4 * 2**20),
        cost_estimate=pl.CostEstimate(flops=0, bytes_accessed=10**6, transcendentals=0),
    )(plan, got_cache0, got_cache1, keys, values)
    picks = shape_of((COLS * requests, ep_count * MOST * COLS), BF16)
    coarse, fine = call(
        weigh_kernel,
        (picks, picks),
        (),
        (),
        (after(expert_ids, rows), gate_weights),
        10**7,
        10**6,
    )
    returned = exchange(after(sums, keys_out, values_out, coarse, fine))
    layer_out = call(
        mix_kernel,
        shape_of((requests, model_width), BF16),
        (),
        (),
        (coarse, fine, summed, returned),
        10**8,
        2 * 10**6,
    )
    return (layer_out, keys_out, values_out)


def solution(mesh):
    rows = P(("dp", "ep"), None)
    caches = P(("dp", "ep"), None, None)
    placed = (
        rows,
        caches,
        caches,
        rows,
        rows,
        P(("dp", "ep")),
        rows,
        rows,
        P(),
        rows,
        rows,
        P("ep", None, "dp"),
        P("ep", None, "dp"),
        P("ep", "dp", None),
    )
    return jax.shard_map(
        local,
        mesh=mesh,
        in_specs=placed,
        out_specs=(rows, caches, caches),
        check_vma=False,
    )
```

```python
import math

import jax
import jax.numpy as jnp
from jax import lax
from jax.experimental import pallas as pl
from jax.experimental.pallas import tpu as pltpu
from jax.sharding import PartitionSpec as P

HD = 128
TOP = 8
MIG = 2
MOST = 2
COLS = 8
STEP = 512
F32 = jnp.float32
BF16 = jnp.bfloat16
VMEM = pl.BlockSpec(memory_space=pltpu.VMEM)
HBM = pl.BlockSpec(memory_space=pltpu.HBM)


def iota(shape, dim):
    return lax.broadcasted_iota(jnp.int32, shape, dim)


def one_hot(condition):
    return jnp.where(condition, 1.0, 0.0).astype(BF16)


def distances(ep_count):
    return tuple(1 + d * (ep_count // 2 - 1) for d in range(MIG))


def find_slot(plan_ref, column, rank, per_device, ep_count):
    found = jnp.int32(0)
    for r in range(per_device):
        other = lax.rem(lax.div(plan_ref[column, r], per_device), ep_count)
        found = jnp.where(other == rank, jnp.int32(r), found)
    return found


def insert_new(lengths_ref, cached_ref, fresh_ref, out_ref):
    requests, slots, width = cached_ref.shape
    fresh = fresh_ref[...].astype(F32)
    position = iota((slots, width), 0)
    for r in range(requests):
        out_ref[r] = jnp.where(
            position == lengths_ref[r], fresh[r : r + 1], cached_ref[r].astype(F32)
        ).astype(BF16)


def store_kernel(
    ep_count,
    lengths_ref,
    plan_ref,
    keys_ref,
    values_ref,
    new_keys_ref,
    new_values_ref,
    keys_out_ref,
    values_out_ref,
    cache0_ref,
    cache1_ref,
):
    requests, slots, _ = keys_ref.shape
    insert_new(lengths_ref, keys_ref, new_keys_ref, keys_out_ref)
    insert_new(lengths_ref, values_ref, new_values_ref, values_out_ref)
    rank = lax.axis_index("ep")
    for distance, cache_ref in zip(distances(ep_count), (cache0_ref, cache1_ref)):
        slot = find_slot(plan_ref, 1, lax.rem(rank + distance, ep_count), requests, ep_count)
        cache_ref[0:slots] = keys_out_ref[slot]
        cache_ref[slots : 2 * slots] = values_out_ref[slot]


def attend_kernel(
    ep_count,
    copies,
    lengths_ref,
    plan_ref,
    queries_ref,
    keys_ref,
    new_keys_ref,
    values_ref,
    new_values_ref,
    residual_ref,
    ids_ref,
    gain_ref,
    carry_ref,
    row0_ref,
    row1_ref,
    keys_out_ref,
    values_out_ref,
):
    requests, slots, width = keys_ref.shape
    heads = queries_ref.shape[1] // HD
    kv_heads = width // HD
    groups = heads // kv_heads
    total = requests * slots
    column = iota((groups * requests, total), 1)
    holder = lax.div(column, slots)
    limit = jnp.zeros_like(column)
    for r in range(requests):
        limit = jnp.where(holder == r, lengths_ref[r], limit)
    own_row = lax.rem(iota((groups * requests, total), 0), requests)
    visible = (holder == own_row) & (lax.rem(column, slots) <= limit)
    for copy in copies[:3]:
        copy.wait()
    insert_new(lengths_ref, keys_ref, new_keys_ref, keys_out_ref)
    queries = queries_ref[...].astype(F32)
    all_keys = keys_out_ref[...].reshape(total, width)
    spread = []
    for k in range(kv_heads):
        stacked = jnp.concatenate(
            [
                queries[:, (k * groups + h) * HD : (k * groups + h + 1) * HD]
                for h in range(groups)
            ],
            axis=0,
        ).astype(BF16)
        scores = lax.dot_general(
            stacked,
            all_keys[:, k * HD : (k + 1) * HD],
            (((1,), (1,)), ((), ())),
            preferred_element_type=F32,
        ) * (1.0 / math.sqrt(HD))
        scores = jnp.where(visible, scores, -jnp.inf)
        weights = jnp.exp(scores - jnp.max(scores, axis=1, keepdims=True))
        spread.append((weights / jnp.sum(weights, axis=1, keepdims=True)).astype(BF16))
    for copy in copies[3:]:
        copy.wait()
    insert_new(lengths_ref, values_ref, new_values_ref, values_out_ref)
    all_values = values_out_ref[...].reshape(total, width)
    residual = residual_ref[...].astype(F32)
    for k, probabilities in enumerate(spread):
        attended = jnp.dot(
            probabilities, all_values[:, k * HD : (k + 1) * HD], preferred_element_type=F32
        )
        for h in range(groups):
            place = slice((k * groups + h) * HD, (k * groups + h + 1) * HD)
            carry_ref[:, place] = (
                residual[:, place] + attended[h * requests : (h + 1) * requests]
            )
    rank = lax.axis_index("ep")
    summed = carry_ref[:, : heads * HD]
    notes = heads * HD + heads * HD // COLS
    row_number = iota(summed.shape, 0)
    for d, (distance, row_ref) in enumerate(zip(distances(ep_count), (row0_ref, row1_ref))):
        slot = find_slot(plan_ref, 1, lax.rem(rank + distance, ep_count), requests, ep_count)
        row_ref[...] = jnp.sum(jnp.where(row_number == slot, summed, 0.0), axis=0, keepdims=True)
        origin = lax.rem(rank + ep_count - distance, ep_count)
        arrival = find_slot(plan_ref, 0, origin, requests, ep_count)
        carry_ref[:, notes + (2 + d) * HD : notes + (3 + d) * HD] = jnp.where(
            iota((requests, HD), 0) == arrival, 1.0, 0.0
        )
    gain = gain_ref[...]
    part = heads * HD // COLS
    carry_ref[:, heads * HD : notes] = jnp.concatenate(
        [gain[:, c * part : (c + 1) * part] for c in range(COLS)], axis=0
    )
    chosen, _, earlier = routes(ids_ref[...], None, ep_count)
    blank = jnp.zeros((requests, HD - ep_count), F32)
    carry_ref[:, notes : notes + HD] = jnp.concatenate([chosen, blank], axis=1)
    carry_ref[:, notes + HD : notes + 2 * HD] = jnp.concatenate([earlier, blank], axis=1)


def routes(ids, gates, experts):
    rows = ids.shape[0]
    expert = iota((rows, experts), 1)
    chosen = jnp.zeros((rows, experts), F32)
    weight = jnp.zeros((rows, experts), F32)
    for k in range(TOP):
        same = ids[:, k : k + 1] == expert
        chosen = jnp.where(same, 1.0, chosen)
        if gates is not None:
            weight = jnp.where(same, gates[:, k : k + 1], weight)
    earlier = []
    running = jnp.zeros((1, experts), F32)
    for r in range(rows):
        earlier.append(running)
        running = running + chosen[r : r + 1]
    return chosen, weight, jnp.concatenate(earlier, axis=0)


def place_kernel(ep_count, carry_ref, row0_ref, row1_ref, summed_out_ref, slots_ref):
    rows, model_width = summed_out_ref.shape
    summed = carry_ref[:, :model_width]
    part = model_width // COLS
    notes = model_width + part
    for d, row_ref in enumerate((row0_ref, row1_ref)):
        arrival = carry_ref[:, notes + (2 + d) * HD : notes + (3 + d) * HD][:, 0:1]
        summed = jnp.where(arrival > 0.5, row_ref[...], summed)
    summed_out_ref[...] = summed
    scale = lax.rsqrt(jnp.mean(summed * summed, axis=1, keepdims=True) + 1e-06)
    scaled = summed * scale
    gain = carry_ref[:, model_width:notes]
    pieces = jnp.concatenate(
        [scaled[:, c * part : (c + 1) * part] * gain[c : c + 1] for c in range(COLS)], axis=0
    ).astype(BF16)
    chosen = carry_ref[:, notes : notes + HD][:, :ep_count]
    earlier = carry_ref[:, notes + HD : notes + 2 * HD][:, :ep_count]
    deep = MOST * COLS
    wide = (ep_count * deep, ep_count)
    spread = one_hot(lax.div(iota(wide, 0), deep) == iota(wide, 1))
    repeat_shape = (rows, COLS * rows)
    repeat = one_hot(iota(repeat_shape, 0) == lax.rem(iota(repeat_shape, 1), rows))
    pick_shape = (ep_count * deep, COLS * rows)
    row_here = iota(pick_shape, 0)
    same_part = lax.rem(row_here, COLS) == lax.div(iota(pick_shape, 1), rows)
    slot_here = lax.rem(lax.div(row_here, COLS), MOST)
    pick = jnp.zeros(pick_shape, F32)
    for s in range(MOST):
        placed = jnp.where(earlier == float(s), chosen, 0.0).astype(BF16)
        by_expert = lax.dot_general(
            placed, repeat, (((0,), (0,)), ((), ())), preferred_element_type=F32
        ).astype(BF16)
        by_piece = jnp.dot(spread, by_expert, preferred_element_type=F32)
        pick = jnp.where(same_part & (slot_here == s), by_piece, pick)
    slots_ref[...] = jnp.dot(pick.astype(BF16), pieces, preferred_element_type=F32).astype(BF16)


def regroup(rows):
    shape = (rows, rows)
    count = rows // COLS
    first = iota(shape, 0)
    return one_hot(
        iota(shape, 1) == lax.rem(first, count) * COLS + lax.div(first, count)
    )


def expert_kernel(n_pieces, n_blocks, cuts, *refs):
    piece_refs = refs[:n_pieces]
    gate_ref, up_ref, down_ref = refs[n_pieces : n_pieces + 3]
    out_refs = refs[n_pieces + 3 : n_pieces + 3 + cuts * n_blocks]
    rows_ref = refs[-1]
    model_width, hidden_width = gate_ref.shape[1:]
    count = STEP // COLS
    part = model_width // COLS
    order = regroup(STEP)
    n = 0
    for ref in piece_refs:
        for m in range(ref.shape[0] // STEP):
            sorted_rows = jnp.dot(
                order, ref[m * STEP : (m + 1) * STEP], preferred_element_type=F32
            ).astype(BF16)
            for c in range(COLS):
                rows_ref[n * count : (n + 1) * count, c * part : (c + 1) * part] = sorted_rows[
                    c * count : (c + 1) * count
                ]
            n += 1
    rows = rows_ref[...]
    gate_proj = jnp.dot(rows, gate_ref[0], preferred_element_type=F32)
    up_proj = jnp.dot(rows, up_ref[0], preferred_element_type=F32)
    hidden = (gate_proj / (1.0 + jnp.exp(-gate_proj)) * up_proj).astype(BF16)
    for c in range(COLS):
        term = jnp.dot(
            hidden, down_ref[0, :, c * part : (c + 1) * part], preferred_element_type=F32
        ).astype(BF16)
        cut, at = divmod(c, COLS // cuts)
        for n in range(n_blocks):
            out_refs[cuts * n + cut][at * count : (at + 1) * count] = term[
                n * count : (n + 1) * count
            ]


def relay_kernel(
    cut, right_ref, left_ref, from_left_ref, from_right_ref, to_right_ref, to_left_ref
):
    rows = from_left_ref.shape[0]
    here = slice(cut * rows, (cut + 1) * rows)
    to_right_ref[...] = (right_ref[here].astype(F32) + from_left_ref[...].astype(F32)).astype(BF16)
    to_left_ref[...] = (left_ref[here].astype(F32) + from_right_ref[...].astype(F32)).astype(BF16)


def gather_kernel(
    own_top_ref,
    own_bottom_ref,
    left_bottom_ref,
    right_top_ref,
    left_first_ref,
    left_second_ref,
    right_first_ref,
    right_second_ref,
    out_ref,
):
    order = regroup(STEP)
    for i, (refs, halves) in enumerate(
        (
            ((own_top_ref, right_top_ref), (left_first_ref, left_second_ref)),
            ((own_bottom_ref, left_bottom_ref), (right_first_ref, right_second_ref)),
        )
    ):
        total = sum(ref[...].astype(F32) for ref in refs)
        total += jnp.concatenate([ref[...].astype(F32) for ref in halves], axis=0)
        out_ref[i * STEP : (i + 1) * STEP] = lax.dot_general(
            order, total.astype(BF16), (((0,), (0,)), ((), ())), preferred_element_type=F32
        ).astype(BF16)


def weigh_kernel(ids_ref, gates_ref, coarse_ref, fine_ref):
    rows, deep = ids_ref.shape[0], MOST * COLS
    experts = coarse_ref.shape[1] // deep
    chosen, weight, earlier = routes(ids_ref[...], gates_ref[...], experts)
    repeat_shape = (COLS * rows, rows)
    repeat = one_hot(lax.rem(iota(repeat_shape, 0), rows) == iota(repeat_shape, 1))
    wide = (experts, experts * deep)
    spread = one_hot(iota(wide, 0) == lax.div(iota(wide, 1), deep))
    pick_shape = (COLS * rows, experts * deep)
    column = iota(pick_shape, 1)
    same_part = lax.div(iota(pick_shape, 0), rows) == lax.rem(column, COLS)
    slot_here = lax.rem(lax.div(column, COLS), MOST)
    picks = [jnp.zeros(pick_shape, F32), jnp.zeros(pick_shape, F32)]
    for s in range(MOST):
        placed = jnp.where((earlier == float(s)) & (chosen > 0.5), weight, 0.0)
        coarse = placed.astype(BF16)
        fine = (placed - coarse.astype(F32)).astype(BF16)
        for i, member in enumerate((coarse, fine)):
            by_row = jnp.dot(
                jnp.dot(repeat, member, preferred_element_type=F32).astype(BF16),
                spread,
                preferred_element_type=F32,
            )
            picks[i] = jnp.where(same_part & (slot_here == s), by_row, picks[i])
    coarse_ref[...] = picks[0].astype(BF16)
    fine_ref[...] = picks[1].astype(BF16)


def mix_kernel(coarse_ref, fine_ref, summed_ref, returned_ref, out_ref):
    rows, model_width = summed_ref.shape
    part = model_width // COLS
    returned = returned_ref[...]
    mixture = jnp.dot(coarse_ref[...], returned, preferred_element_type=F32)
    mixture += jnp.dot(fine_ref[...], returned, preferred_element_type=F32)
    for c in range(COLS):
        here = slice(c * part, (c + 1) * part)
        out_ref[:, here] = (
            summed_ref[:, here] + mixture[c * rows : (c + 1) * rows]
        ).astype(BF16)


def settle_kernel(
    ep_count,
    plan_ref,
    cache0_ref,
    cache1_ref,
    keys_in_ref,
    values_in_ref,
    keys_ref,
    values_ref,
    sems,
):
    del keys_in_ref, values_in_ref
    requests, slots, _ = keys_ref.shape
    rank = lax.axis_index("ep")
    copies = []
    for d, (distance, cache_ref) in enumerate(zip(distances(ep_count), (cache0_ref, cache1_ref))):
        origin = lax.rem(rank + ep_count - distance, ep_count)
        slot = find_slot(plan_ref, 0, origin, requests, ep_count)
        for i, ref in enumerate((keys_ref, values_ref)):
            copies.append(
                pltpu.make_async_copy(
                    cache_ref.at[pl.ds(i * slots, slots)], ref.at[slot], sems.at[d, i]
                )
            )
            copies[-1].start()
    for copy in copies:
        copy.wait()


def shape_of(shape, dtype):
    return jax.ShapeDtypeStruct(shape, dtype)


def call(kernel, outs, scalars, staged, resident, flops, moved, limit=16, scratch=(), lazy=False):
    n_scalars, n_staged, n_resident = map(len, (scalars, staged, resident))
    n_outs = len(outs) if isinstance(outs, tuple) else 1

    def body(*refs):
        refs = list(refs)

        def take(count):
            taken = refs[:count]
            del refs[:count]
            return taken

        scalar_refs, sources, resident_refs, out_refs = map(
            take, (n_scalars, n_staged, n_resident, n_outs)
        )
        own_refs = take(len(scratch))
        staged_refs = take(n_staged)
        copies = [
            pltpu.make_async_copy(source, target, refs[0].at[i])
            for i, (source, target) in enumerate(zip(sources, staged_refs))
        ]
        for copy in copies:
            copy.start()
        if not lazy:
            for copy in copies:
                copy.wait()
        first = (copies,) if lazy else ()
        kernel(*first, *scalar_refs, *staged_refs, *resident_refs, *out_refs, *own_refs)

    stages = [pltpu.VMEM(arg.shape, arg.dtype) for arg in staged]
    if staged:
        stages.append(pltpu.SemaphoreType.DMA((n_staged,)))
    return pl.pallas_call(
        body,
        out_shape=outs,
        grid_spec=pltpu.PrefetchScalarGridSpec(
            num_scalar_prefetch=n_scalars,
            grid=(),
            in_specs=[HBM] * n_staged + [VMEM] * n_resident,
            out_specs=tuple([VMEM] * n_outs) if isinstance(outs, tuple) else VMEM,
            scratch_shapes=[*scratch, *stages],
        ),
        compiler_params=pltpu.CompilerParams(vmem_limit_bytes=limit * 2**20),
        cost_estimate=pl.CostEstimate(flops=flops, bytes_accessed=moved, transcendentals=0),
    )(*scalars, *staged, *resident)


def experts_of(pieces, weights, cuts=1):
    rows = sum(piece.shape[0] for piece in pieces)
    part = pieces[0].shape[1]
    n_blocks = rows // STEP
    model_width, hidden_width = weights[0].shape[1:]
    tokens = rows // COLS

    def kernel(*refs):
        expert_kernel(len(pieces), n_blocks, cuts, *refs)

    return call(
        kernel,
        tuple(shape_of((STEP // cuts, part), BF16) for _ in range(cuts * n_blocks)),
        (),
        (),
        (*pieces, *weights),
        6 * tokens * model_width * hidden_width,
        6 * model_width * hidden_width + 4 * rows * part,
        limit=20,
        scratch=[pltpu.VMEM((tokens, model_width), BF16)],
    )


def rotate(member, axis, distance):
    count = lax.axis_size(axis)
    return lax.ppermute(member, axis, [(s, (s + distance) % count) for s in range(count)])


def exchange(member):
    experts = lax.axis_size("ep")
    cut = member.reshape(experts, member.shape[0] // experts, member.shape[1])
    cut = lax.all_to_all(cut, "ep", split_axis=0, concat_axis=0, tiled=True)
    return cut.reshape(member.shape)


def after(member, *earlier):
    return lax.optimization_barrier((member, *earlier))[0]


def through_experts(own, weights, beside):
    top, bottom = own[:STEP], own[STEP:]
    left_rows_top = rotate(top, "dp", 1)
    right_rows_bottom = rotate(bottom, "dp", -1)
    left_rows_bottom = rotate(bottom, "dp", 1)
    right_rows_top = rotate(top, "dp", -1)
    own_top, own_bottom = experts_of([own], weights)
    one, other, distance = beside
    left_rows_top, right_rows_bottom, own_top, own_bottom, one, other = lax.optimization_barrier(
        (left_rows_top, right_rows_bottom, own_top, own_bottom, one, other)
    )
    other = rotate(other, "ep", distance)
    far_top = rotate(left_rows_top, "dp", 1)
    far_bottom = rotate(right_rows_bottom, "dp", -1)
    left_rows_bottom, right_rows_top, other = lax.optimization_barrier(
        (left_rows_bottom, right_rows_top, other)
    )
    left_top, left_bottom, right_top, right_bottom = experts_of(
        [left_rows_top, left_rows_bottom, right_rows_top, right_rows_bottom], weights
    )
    direct_left = rotate(right_bottom, "dp", 1)
    direct_right = rotate(left_top, "dp", -1)
    far_top, far_bottom, right_top, left_bottom = lax.optimization_barrier(
        (far_top, far_bottom, right_top, left_bottom)
    )
    far_terms = experts_of([far_top, far_bottom], weights, cuts=2)
    size = 2 * right_top.size
    part = right_top.shape[1]
    block = shape_of((STEP // 2, part), BF16)
    sums_left, sums_right = [], []
    to_right, to_left = direct_left, direct_right
    for cut in range(2):
        relayed_left = rotate(far_terms[cut], "dp", 1)
        relayed_right = rotate(far_terms[2 + cut], "dp", -1)
        if cut:
            sums_left.append(rotate(to_right, "dp", 1))
            sums_right.append(rotate(to_left, "dp", -1))
        relayed_left, relayed_right, *_ = lax.optimization_barrier(
            (relayed_left, relayed_right, to_right, to_left)
        )

        def relay(*refs, cut=cut):
            relay_kernel(cut, *refs)

        to_right, to_left = call(
            relay,
            (block, block),
            (),
            (),
            (right_top, left_bottom, relayed_left, relayed_right),
            size,
            5 * size,
        )
    sums_left.append(rotate(to_right, "dp", 1))
    sums_right.append(rotate(to_left, "dp", -1))
    sums = call(
        gather_kernel,
        shape_of((2 * STEP, part), BF16),
        (),
        (),
        (own_top, own_bottom, direct_left, direct_right, *sums_left, *sums_right),
        2 * size * STEP,
        8 * size,
    )
    return sums, one, other


def local(
    queries,
    key_cache,
    value_cache,
    new_keys,
    new_values,
    cache_lengths,
    residual,
    move_plan,
    norm_gain,
    expert_ids,
    gate_weights,
    w_gate,
    w_up,
    w_down,
):
    requests, model_width = queries.shape
    slots, width = key_cache.shape[1:]
    ep_count = lax.axis_size("ep")
    plan = move_plan.T
    cache = shape_of(key_cache.shape, BF16)
    row = shape_of((1, model_width), F32)
    moving = shape_of((2 * slots, width), BF16)
    summed_shape = shape_of((requests, model_width), F32)
    steps = distances(ep_count)

    def attend(*refs):
        attend_kernel(ep_count, *refs)

    carry, row0, row1 = call(
        attend,
        (shape_of((requests, model_width + model_width // COLS + 4 * HD), F32), row, row),
        (cache_lengths, plan),
        (
            queries,
            key_cache,
            new_keys,
            value_cache,
            new_values,
            residual,
            expert_ids,
            norm_gain.reshape(1, model_width),
        ),
        (),
        10**8,
        3 * 10**6,
        limit=58,
        lazy=True,
        scratch=[pltpu.VMEM(cache.shape, BF16), pltpu.VMEM(cache.shape, BF16)],
    )
    got_row0 = rotate(row0, "ep", steps[0])
    got_row1 = rotate(row1, "ep", steps[1])

    def place(*refs):
        place_kernel(ep_count, *refs)

    part = model_width // COLS
    summed, outgoing = call(
        place,
        (summed_shape, shape_of((ep_count * MOST * COLS, part), BF16)),
        (),
        (),
        (carry, got_row0, got_row1),
        10**8,
        2 * 10**6,
    )
    rows = exchange(outgoing)

    def store(*refs):
        store_kernel(ep_count, *refs)

    keys, values, cache0, cache1 = call(
        store,
        (cache, cache, moving, moving),
        (cache_lengths, plan),
        (after(key_cache, rows), value_cache, new_keys, new_values),
        (),
        0,
        3 * 10**6,
    )
    got_cache0 = rotate(cache0, "ep", steps[0])

    def settle(*refs):
        settle_kernel(ep_count, *refs)

    sums, got_cache0, got_cache1 = through_experts(
        rows, (w_gate, w_up, w_down), (got_cache0, cache1, steps[1])
    )
    keys_out, values_out = pl.pallas_call(
        settle,
        out_shape=(cache, cache),
        grid_spec=pltpu.PrefetchScalarGridSpec(
            num_scalar_prefetch=1,
            grid=(),
            in_specs=[VMEM, VMEM, HBM, HBM],
            out_specs=(HBM, HBM),
            scratch_shapes=[pltpu.SemaphoreType.DMA((MIG, 2))],
        ),
        input_output_aliases={3: 0, 4: 1},
        compiler_params=pltpu.CompilerParams(vmem_limit_bytes=4 * 2**20),
        cost_estimate=pl.CostEstimate(flops=0, bytes_accessed=10**6, transcendentals=0),
    )(plan, got_cache0, got_cache1, keys, values)
    picks = shape_of((COLS * requests, ep_count * MOST * COLS), BF16)
    coarse, fine = call(
        weigh_kernel,
        (picks, picks),
        (),
        (),
        (after(expert_ids, rows), gate_weights),
        10**7,
        10**6,
    )
    returned = exchange(after(sums, keys_out, values_out, coarse, fine))
    layer_out = call(
        mix_kernel,
        shape_of((requests, model_width), BF16),
        (),
        (),
        (coarse, fine, summed, returned),
        10**8,
        2 * 10**6,
    )
    return (layer_out, keys_out, values_out)


def solution(mesh):
    rows = P(("dp", "ep"), None)
    caches = P(("dp", "ep"), None, None)
    placed = (
        rows,
        caches,
        caches,
        rows,
        rows,
        P(("dp", "ep")),
        rows,
        rows,
        P(),
        rows,
        rows,
        P("ep", None, "dp"),
        P("ep", None, "dp"),
        P("ep", "dp", None),
    )
    return jax.shard_map(
        local,
        mesh=mesh,
        in_specs=placed,
        out_specs=(rows, caches, caches),
        check_vma=False,
    )
```
